32 devices in a mesh: dp: 2 (over core), seq: 4 (over y, x), tensor: 4 (over z).
Axes of the slice: x: 2, y: 2, z: 4, core: 2. Of those that a mesh axis runs over, the one named last changes fastest.
Arguments:
- tokens: bfloat16 [2, 4096, 512], P('dp', 'seq'), may hold values from -6 to 6
- levels: int32 [2, 4096], P('dp', 'seq'), may hold values from 0 to 255
- boundaries: int32 [2, 32], P('dp', 'seq'), may hold values from 0 to 255
- level_table: float32 [256, 512], replicated, may hold values from -6 to 6
- w_key: bfloat16 [512, 1024], P(None, 'tensor'), as said below
- w_value: bfloat16 [512, 1024], P(None, 'tensor'), may hold values from -0.25 to 0.25
- slopes: float32 [8], P('tensor'), may hold values from 0.003 to 0.3
- queries: bfloat16 [2, 1024, 1024], P('dp', 'seq', 'tensor'), may hold values from -6 to 6
- cotangent: bfloat16 [2, 1024, 1024], P('dp', 'seq', 'tensor'), may hold values from -6 to 6
Outputs:
- attended: bfloat16 [2, 1024, 1024], P('dp', 'seq', 'tensor')
- query_grad: bfloat16 [2, 1024, 1024], P('dp', 'seq', 'tensor')
- key_weight_grad: float32 [512, 1024], P(('dp', 'seq'), 'tensor')
- value_weight_grad: float32 [512, 1024], P(('dp', 'seq'), 'tensor')
- slope_grad: float32 [8], P('tensor')
The draws below stay inside these ranges and needn't reach their ends.
Inputs may be any that keep to these rules, and one draw needn't show every extreme that they name: `boundaries`: a value of 128 or more means that no episode starts in the block. `w_key`: entries lie within 6 / sqrt(512) of zero.
All inputs are finite; a program needn't handle non-finite values.
Results may differ from the reference program's by a relative error of at most 0.0045.
The reference program's roundings to bfloat16 on the way count: a program that leaves them out, or rounds other values in their place, can miss the bound.
Values may be sent and summed in bfloat16 or wider, within the bound.
No kernel may reach another device: no remote copies, remote signals or barrier semaphores. Data moves between devices by JAX's collectives and lax.ppermute only.
A program may use at most 64 MiB of HBM per device.

```python
import math
import jax
import jax.numpy as jnp
from jax import lax

N_LAT = 1024
HEADS = 8
HEAD = 128
C = 512
LEVELS = 256
BLOCK = 128
SEQLEN = 4096
TRAJ = 2


def draw_level_table(key, part):
    key = jax.random.fold_in(key, 21)
    first = jax.random.fold_in(key, 0)
    table = jnp.clip(jax.random.normal(first, (LEVELS, C), jnp.float32), -6.0, 6.0)
    return table.astype(jnp.float32)


def draw_w_key(key, part):
    key = jax.random.fold_in(key, 22)
    spread = 1.0 / math.sqrt(C)
    weight = jnp.clip(jax.random.normal(key, (C, HEADS * HEAD), jnp.float32) * spread, -6.0 * spread, 6.0 * spread)
    return weight.astype(jnp.bfloat16)


def draw_queries(key, part):
    key = jax.random.fold_in(key, 23)
    first = jax.random.fold_in(key, 0)
    shape = (TRAJ, N_LAT, HEADS * HEAD)
    result = jnp.clip(jax.random.normal(first, shape, jnp.float32), -6.0, 6.0)
    return result.astype(jnp.bfloat16)


def touch_ends(entries, key, low, largest):
    place = [jax.random.randint(jax.random.fold_in(key, axis), (), 0, length) for axis, length in enumerate(entries.shape)]
    longest = entries.shape.index(max(entries.shape))
    next_to = place[:longest] + [(place[longest] + 1) % entries.shape[longest]] + place[longest + 1:]
    return entries.at[tuple(place)].set(low).at[tuple(next_to)].set(largest)


def steps_of(key, shape, cuts, least, top_value):
    def one(dim, parts):
        draws = jax.random.uniform(jax.random.fold_in(jax.random.fold_in(key, 6), dim), (parts,), jnp.float32, least / len(cuts), top_value / len(cuts))
        return jnp.repeat(jnp.exp(draws), shape[dim] // parts).reshape((-1,) + (1,) * (len(shape) - dim - 1))

    level = one(*cuts[0])
    for cut in cuts[1:]:
        level = level * one(*cut)
    return level


def scatter_about(stream_key, shape, scale, limit, cuts=(), held_as=jnp.bfloat16):
    values = jax.random.normal(stream_key, shape, jnp.float32) * scale
    if len(cuts) > 0:
        values = steps_of(stream_key, shape, cuts, -0.22, 0.18) * values
    return jnp.clip(values, min=-limit, max=limit).astype(held_as)


def setup_inputs(seed: int = 0) -> dict:
    streams_of = jax.random.split(jax.random.key(seed), 10)
    tokens = scatter_about(streams_of[0], (TRAJ, SEQLEN, C), 1.0, 6.0, ((0, 2), (1, 4)))
    levels = touch_ends(jax.random.randint(streams_of[1], (TRAJ, SEQLEN), 0, LEVELS), jax.random.fold_in(streams_of[1], 1), 0, LEVELS - 1).astype(jnp.int32)
    boundaries = touch_ends(jax.random.randint(streams_of[2], (TRAJ, SEQLEN // BLOCK), 0, 2 * BLOCK), jax.random.fold_in(streams_of[2], 1), 0, (2 * BLOCK) - 1).astype(jnp.int32)
    level_table = draw_level_table(jax.random.fold_in(streams_of[9], 71), 0)
    w_key = draw_w_key(jax.random.fold_in(streams_of[9], 71), 0)
    w_value = scatter_about(streams_of[5], (C, HEADS * HEAD), C ** -0.5, 0.25, ((1, 4),))
    slopes = jnp.clip(jnp.exp(math.log(0.3) - 4.6051702 * jax.random.uniform(streams_of[6], (HEADS,), jnp.float32) ** steps_of(streams_of[6], (HEADS,), ((0, 4),), -0.2, 0.2)), 0.003, 0.3)
    queries = draw_queries(jax.random.fold_in(streams_of[9], 71), 0)
    cotangent = scatter_about(streams_of[8], (TRAJ, N_LAT, HEADS * HEAD), 1.0, 6.0, ((0, 2), (1, 4), (2, 4)))
    return dict(tokens=tokens, levels=levels, boundaries=boundaries, level_table=level_table, w_key=w_key, w_value=w_value, slopes=slopes, queries=queries, cotangent=cotangent)


def episode_index(bounds):
    has = (bounds < BLOCK).astype(jnp.int32)
    before = jnp.cumsum(has) - has
    position = jnp.arange(BLOCK, dtype=jnp.int32)
    inside = (position[None, :] >= bounds[:, None]).astype(jnp.int32)
    return (before[:, None] + inside).reshape(-1)

def reference(tokens, levels, boundaries, level_table, w_key, w_value, slopes, queries, cotangent):
    scale = HEAD ** (-0.5)
    block_rows = min(4096, SEQLEN)
    count = SEQLEN // block_rows
    feats = HEADS * HEAD
    attended_all = []
    query_all = []
    grad_key = jnp.zeros((C, feats), jnp.float32)
    grad_value = jnp.zeros((C, feats), jnp.float32)
    grad_slope = jnp.zeros((HEADS,), jnp.float32)
    for traj in range(TRAJ):
        raw = tokens[traj].astype(jnp.float32)
        centered = raw - lax.optimization_barrier(jnp.mean(raw, axis=1, keepdims=True))
        normed = centered / jnp.sqrt(lax.optimization_barrier(jnp.mean(centered * centered, axis=1, keepdims=True)) + 1e-05)
        inputs = (normed + level_table[levels[traj]]).astype(jnp.bfloat16)
        keys = jnp.dot(inputs, w_key, preferred_element_type=jnp.float32).astype(jnp.bfloat16)
        values = jnp.dot(inputs, w_value, preferred_element_type=jnp.float32).astype(jnp.bfloat16)
        episode = episode_index(boundaries[traj]).astype(jnp.float32)
        query = queries[traj].astype(jnp.float32).reshape(N_LAT, HEADS, HEAD)
        grad_out = cotangent[traj].astype(jnp.float32).reshape(N_LAT, HEADS, HEAD).transpose(1, 0, 2)
        key_blocks = keys.reshape(count, block_rows, HEADS, HEAD)
        value_blocks = values.reshape(count, block_rows, HEADS, HEAD)
        episode_blocks = episode.reshape(count, block_rows)
        input_blocks = inputs.reshape(count, block_rows, C)

        def scores(kblock, eblock):
            return jnp.einsum('nhd,thd->hnt', query, kblock.astype(jnp.float32)) * scale + slopes[:, None, None] * eblock[None, None, :]

        def max_step(carry, item):
            kblock, eblock = item
            return (jnp.maximum(carry, lax.optimization_barrier(jnp.max(scores(kblock, eblock), axis=2))), None)
        top, _ = lax.scan(max_step, jnp.full((HEADS, N_LAT), -jnp.inf, jnp.float32), (key_blocks, episode_blocks))

        def sum_step(carry, item):
            kblock, vblock, eblock = item
            expo = jnp.exp(scores(kblock, eblock) - top[:, :, None])
            weights = expo.astype(jnp.bfloat16).astype(jnp.float32)
            acc = carry[0] + jnp.einsum('hnt,thd->hnd', weights, vblock.astype(jnp.float32))
            return ((acc, carry[1] + lax.optimization_barrier(jnp.sum(expo, axis=2))), None)
        zero_acc = jnp.zeros((HEADS, N_LAT, HEAD), jnp.float32)
        (acc, total), _ = lax.scan(sum_step, (zero_acc, jnp.zeros((HEADS, N_LAT), jnp.float32)), (key_blocks, value_blocks, episode_blocks))
        mixed = acc / total[:, :, None]
        attended_all.append(mixed.transpose(1, 0, 2).reshape(N_LAT, feats).astype(jnp.bfloat16))
        delta = lax.optimization_barrier(jnp.sum(grad_out * mixed, axis=2))

        def grad_step(carry, item):
            dq, dwk, dwv, dsl = carry
            kblock, vblock, eblock, xblock = item
            probs = jnp.exp(scores(kblock, eblock) - top[:, :, None]) / total[:, :, None]
            probs_b = probs.astype(jnp.bfloat16).astype(jnp.float32)
            dv = jnp.einsum('hnt,hnd->thd', probs_b, grad_out).astype(jnp.bfloat16).reshape(block_rows, feats)
            dprod = jnp.einsum('hnd,thd->hnt', grad_out, vblock.astype(jnp.float32))
            sgrad = probs * (dprod - delta[:, :, None])
            dsl = dsl + lax.optimization_barrier(jnp.sum(sgrad * eblock[None, None, :], axis=(1, 2)))
            sgrad_b = sgrad.astype(jnp.bfloat16).astype(jnp.float32)
            dq = dq + scale * jnp.einsum('hnt,thd->hnd', sgrad_b, kblock.astype(jnp.float32))
            dk = (scale * jnp.einsum('hnt,nhd->thd', sgrad_b, query)).astype(jnp.bfloat16).reshape(block_rows, feats)
            dwk = dwk + jnp.dot(xblock.T, dk, preferred_element_type=jnp.float32)
            dwv = dwv + jnp.dot(xblock.T, dv, preferred_element_type=jnp.float32)
            return ((dq, dwk, dwv, dsl), None)
        init = (zero_acc, grad_key, grad_value, grad_slope)
        (dq, grad_key, grad_value, grad_slope), _ = lax.scan(grad_step, init, (key_blocks, value_blocks, episode_blocks, input_blocks))
        query_all.append(dq.transpose(1, 0, 2).reshape(N_LAT, feats).astype(jnp.bfloat16))
    return (jnp.stack(attended_all), jnp.stack(query_all), grad_key, grad_value, grad_slope)
```

```python
import functools

import jax
import jax.numpy as jnp
from jax import lax
from jax.experimental import pallas as pl
from jax.experimental.pallas import tpu as pltpu
from jax.sharding import PartitionSpec as P

HEAD = 128
BLOCK = 128
LOG2E = 1.4426950408889634
CODE_MAX = 32000.0
TINY = 1e-30
CHUNK = 256

F32 = jnp.float32
BF16 = jnp.bfloat16
I16 = jnp.int16
VMEM = pl.BlockSpec(memory_space=pltpu.VMEM)
SMEM = pl.BlockSpec(memory_space=pltpu.SMEM)


def nn(a, b):
    return lax.dot_general(a, b, (((1,), (0,)), ((), ())), preferred_element_type=F32)


def nt(a, b):
    return lax.dot_general(a, b, (((1,), (1,)), ((), ())), preferred_element_type=F32)


def tn(a, b):
    return lax.dot_general(a, b, (((0,), (0,)), ((), ())), preferred_element_type=F32)


def head_cols(h):
    return slice(h * HEAD, (h + 1) * HEAD)


def swap(x, axis, k, n):
    return lax.ppermute(x, axis, [(i, i ^ k) for i in range(n)])


def encode(x):
    most = jnp.maximum(jnp.max(jnp.abs(x), axis=0, keepdims=True), TINY)
    exponent = jnp.ceil(jnp.log2(most))
    steps = jnp.round(x * (jnp.exp2(-exponent) * CODE_MAX))
    return steps, exponent


def decode(steps, exponent):
    return steps.astype(jnp.int32).astype(F32) * (jnp.exp2(exponent.astype(jnp.int32).astype(F32)) * (1.0 / CODE_MAX))


def to_code(x):
    return x.astype(jnp.int32).astype(I16)


def stack_rows(rows, total, width):
    place = lax.broadcasted_iota(jnp.int32, (total, width), 0)
    out = jnp.zeros((total, width), F32)
    for i, row in enumerate(rows):
        out = jnp.where(place == i, row, out)
    return out


def prep_kernel(tok_ref, lev_ref, table_ref, wk_ref, wv_ref, inp_ref, key_ref, val_ref):
    table = table_ref[...]
    hi = table.astype(BF16)
    rest = table - hi.astype(F32)
    mid = rest.astype(BF16)
    low = (rest - mid.astype(F32)).astype(BF16)
    levels = table.shape[0]
    for c in range(tok_ref.shape[1] // CHUNK):
        rows = slice(c * CHUNK, (c + 1) * CHUNK)
        raw = tok_ref[0, rows, :].astype(F32)
        centered = raw - jnp.mean(raw, axis=1, keepdims=True)
        normed = centered / jnp.sqrt(jnp.mean(centered * centered, axis=1, keepdims=True) + 1e-05)
        ids = lev_ref[0:1, rows]
        pick = (lax.broadcasted_iota(jnp.int32, (levels, CHUNK), 0) == ids).astype(F32).astype(BF16)
        lookup = (tn(pick, low) + tn(pick, mid)) + tn(pick, hi)
        inputs = (normed + lookup).astype(BF16)
        inp_ref[rows, :] = inputs
        key_ref[rows, :] = nn(inputs, wk_ref[...]).astype(BF16)
        val_ref[rows, :] = nn(inputs, wv_ref[...]).astype(BF16)


def fill_episode(bounds_ref, episode_ref, base):
    before = jnp.int32(0)
    place = lax.broadcasted_iota(jnp.int32, (BLOCK, 128), 0)
    for b in range(bounds_ref.shape[1]):
        bound = bounds_ref[0, b]
        local = before + (place >= bound).astype(jnp.int32)
        episode_ref[b * BLOCK : (b + 1) * BLOCK, :] = base + local.astype(F32)
        before = before + (bound < BLOCK).astype(jnp.int32)
    return before


def wide(column, width):
    return jnp.concatenate([column] * (width // 128), axis=1)


def top_kernel(n, bounds_ref, slopes_ref, key_ref, *refs):
    q_refs, (stats_ref, episode_ref) = refs[:n], refs[n:]
    rows = q_refs[0].shape[1]
    tokens, width = key_ref.shape
    heads = width // HEAD
    starts = fill_episode(bounds_ref, episode_ref, 0.0)
    scale = HEAD ** (-0.5)
    tops = []
    for h in range(heads):
        for j in range(n):
            best = None
            query = q_refs[j][0, :, head_cols(h)]
            for c in range(tokens // CHUNK):
                part = slice(c * CHUNK, (c + 1) * CHUNK)
                score = nt(key_ref[part, head_cols(h)], query) * scale
                score = score + wide(slopes_ref[h] * episode_ref[part, :], rows)
                most = jnp.max(score, axis=0, keepdims=True)
                best = most if best is None else jnp.maximum(best, most)
            tops.append(best)
    tops.append(jnp.zeros((1, rows), F32) + starts.astype(F32))
    stats_ref[...] = stack_rows(tops, stats_ref.shape[0], rows)


def merged_tops(n, heads, slopes_ref, stats_refs):
    me = lax.axis_index("seq")
    counts = [ref[heads * n : heads * n + 1, :] for ref in stats_refs]
    bases = []
    for k in range(n):
        base = jnp.zeros_like(counts[0])
        for j in range(n):
            earlier = ((me ^ j) < (me ^ k)).astype(F32)
            base = base + earlier * counts[j]
        bases.append(base)
    tops = []
    for h in range(heads):
        row = []
        for j in range(n):
            best = None
            for k in range(n):
                place = h * n + (j ^ k)
                top = stats_refs[k][place : place + 1, :] + slopes_ref[h] * bases[k]
                best = top if best is None else jnp.maximum(best, top)
            row.append(best)
        tops.append(row)
    return tops, bases[0]


def gather_blocks(refs, scratch):
    rows = refs[0].shape[1]
    for j, ref in enumerate(refs):
        scratch[j * rows : (j + 1) * rows, :] = ref[0]


def sums_kernel(n, bounds_ref, slopes_ref, key_ref, val_ref, *refs):
    q_refs, g_refs, top_refs = refs[:n], refs[n : 2 * n], refs[2 * n : 3 * n]
    stats_ref, own_ref = refs[3 * n : 3 * n + 2]
    send_refs = refs[3 * n + 2 : 4 * n + 1]
    episode_ref, q_all, g_all, out_ref = refs[4 * n + 1 :]
    rows = q_refs[0].shape[1]
    tokens, width = key_ref.shape
    heads = width // HEAD
    scale = HEAD ** (-0.5)
    tops, base = merged_tops(n, heads, slopes_ref, top_refs)
    fill_episode(bounds_ref, episode_ref, base[:, :128])
    gather_blocks(q_refs, q_all)
    gather_blocks(g_refs, g_all)
    lats = n * rows
    norms, deltas = [], []
    for h in range(heads):
        top = jnp.concatenate(tops[h], axis=1)

        def step(c, carry):
            norm, delta = carry
            part = pl.ds(pl.multiple_of(c * CHUNK, CHUNK), CHUNK)
            keys, values = key_ref[part, head_cols(h)], val_ref[part, head_cols(h)]
            score = nt(keys, q_all[:, head_cols(h)]) * scale
            score = score + wide(slopes_ref[h] * episode_ref[part, :], lats)
            expo = jnp.exp(score - top)
            weights = expo.astype(BF16)
            dprod = nt(values, g_all[:, head_cols(h)])
            out_ref[...] += tn(values, weights)
            norm = norm + jnp.sum(expo, axis=0, keepdims=True)
            delta = delta + jnp.sum(weights.astype(F32) * dprod, axis=0, keepdims=True)
            return norm, delta

        out_ref[...] = jnp.zeros_like(out_ref)
        zero = jnp.zeros((1, lats), F32)
        norm, delta = lax.fori_loop(0, tokens // CHUNK, step, (zero, zero))
        norms += [norm[:, j * rows : (j + 1) * rows] for j in range(n)]
        deltas += [delta[:, j * rows : (j + 1) * rows] for j in range(n)]
        own_ref[head_cols(h), :] = out_ref[:, :rows]
        write_messages(h, n, rows, heads, out_ref, send_refs)
    stats_ref[...] = stack_rows(norms + deltas, stats_ref.shape[0], rows)


def write_messages(h, n, rows, heads, sums_ref, send_refs):
    for j in range(1, n):
        steps, exponent = encode(sums_ref[:, j * rows : (j + 1) * rows])
        send_refs[j - 1][head_cols(h), :] = to_code(steps)
        place = (heads + h * 0) * HEAD + h * 16
        send_refs[j - 1][place : place + 16, :] = to_code(jnp.broadcast_to(exponent, (16, rows)))


def read_message(ref, h, heads):
    place = heads * HEAD + h * 16
    return decode(ref[head_cols(h), :], ref[place : place + 16, :][0:1, :])


def merged_sums(n, heads, stats_refs):
    norms, deltas = [], []
    for h in range(heads):
        norm_row, delta_row = [], []
        for j in range(n):
            norm = delta = None
            for k in range(n):
                place = h * n + (j ^ k)
                a = stats_refs[k][place : place + 1, :]
                b = stats_refs[k][heads * n + place : heads * n + place + 1, :]
                norm = a if norm is None else norm + a
                delta = b if delta is None else delta + b
            norm_row.append(norm)
            delta_row.append(delta)
        norms.append(jnp.concatenate(norm_row, axis=1))
        deltas.append(jnp.concatenate(delta_row, axis=1))
    return norms, deltas


def grads_kernel(n, bounds_ref, slopes_ref, inp_ref, key_ref, val_ref, *refs):
    q_refs, g_refs, top_refs, sum_refs = (refs[i * n : (i + 1) * n] for i in range(4))
    own_ref, keep_ref, give_ref = refs[4 * n : 4 * n + 3]
    send_refs = refs[4 * n + 3 : 5 * n + 2]
    episode_ref, q_all, g_all, dq_ref, tok_ref, weight_ref = refs[5 * n + 2 :]
    rows = q_refs[0].shape[1]
    tokens, width = key_ref.shape
    heads = width // HEAD
    scale = HEAD ** (-0.5)
    tops, base = merged_tops(n, heads, slopes_ref, top_refs)
    norms, deltas = merged_sums(n, heads, sum_refs)
    fill_episode(bounds_ref, episode_ref, base[:, :128])
    gather_blocks(q_refs, q_all)
    gather_blocks(g_refs, g_all)
    lats = n * rows
    slope_rows = []
    for h in range(heads):
        top = jnp.concatenate(tops[h], axis=1)
        inverse = 1.0 / norms[h]
        mean = deltas[h] * inverse

        def step(c, slope):
            part = pl.ds(pl.multiple_of(c * CHUNK, CHUNK), CHUNK)
            keys, values = key_ref[part, head_cols(h)], val_ref[part, head_cols(h)]
            query, grad = q_all[:, head_cols(h)], g_all[:, head_cols(h)]
            episode = wide(episode_ref[part, :], lats)
            score = nt(keys, query) * scale
            score = score + slopes_ref[h] * episode
            probs = jnp.exp(score - top) * inverse
            tok_ref[part, width + h * HEAD : width + (h + 1) * HEAD] = nn(probs.astype(BF16), grad).astype(BF16)
            dprod = nt(values, grad)
            score_grad = probs * (dprod - mean)
            slope = slope + jnp.sum(score_grad * episode, axis=0, keepdims=True)
            score_grad_b = score_grad.astype(BF16)
            tok_ref[part, head_cols(h)] = (scale * nn(score_grad_b, query)).astype(BF16)
            dq_ref[...] += tn(keys, score_grad_b)
            return slope

        dq_ref[...] = jnp.zeros_like(dq_ref)
        slope = lax.fori_loop(0, tokens // CHUNK, step, jnp.zeros((1, lats), F32))
        slope_rows.append(jnp.sum(slope, axis=1, keepdims=True))
        own_ref[head_cols(h), :] = dq_ref[:, :rows]
        write_messages(h, n, rows, heads, dq_ref, send_refs)
    half = keep_ref.shape[0] - 8
    weight_ref[0] = tn(inp_ref[:, :half], tok_ref[...])
    weight_ref[1] = tn(inp_ref[:, half:], tok_ref[...])
    core = lax.axis_index("dp")
    keep_ref[:half, :] = weight_ref[core]
    give_ref[:half, :] = weight_ref[1 - core]
    columns = keep_ref.shape[1]
    slopes = stack_rows([jnp.broadcast_to(s, (1, columns)) for s in slope_rows], 8, columns)
    keep_ref[half:, :] = slopes
    give_ref[half:, :] = slopes


def pair_kernel(n, heads, keep_ref, got_ref, own_ref, *send_refs):
    me = lax.axis_index("seq")
    half = keep_ref.shape[0] - 8
    piece = half // n
    width = keep_ref.shape[1]
    place = lax.broadcasted_iota(jnp.int32, (16, width), 0)
    slopes = keep_ref[half:, :] + got_ref[half:, :]
    digits = []
    for h in range(heads):
        value = slopes[h : h + 1, :]
        steps, exponent = encode(value)
        left = value * (jnp.exp2(-exponent) * CODE_MAX) - steps
        digits += [exponent, steps, jnp.round(left * CODE_MAX)]
    for k in range(n):
        rows = pl.ds(pl.multiple_of((me ^ k) * piece, piece), piece)
        total = keep_ref[rows, :] + got_ref[rows, :]
        if k == 0:
            own_ref[:piece, :] = total
            own_ref[piece:, :] = slopes
        else:
            steps, exponent = encode(total)
            send_refs[k - 1][:piece, :] = to_code(steps)
            send_refs[k - 1][piece:, :] = to_code(stack_rows([exponent] + digits, 16, width))


def attended_kernel(n, heads, own_ref, *refs):
    got_refs, sum_refs, out_ref = refs[: n - 1], refs[n - 1 : 2 * n - 1], refs[2 * n - 1]
    rows = own_ref.shape[1]
    norms, _ = merged_sums(n, heads, sum_refs)
    for h in range(heads):
        total = own_ref[head_cols(h), :]
        for ref in got_refs:
            total = total + read_message(ref, h, heads)
        total = total / norms[h][:, :rows]
        out_ref[0, :, head_cols(h)] = total.T.astype(BF16)


def last_kernel(n, heads, own_ref, weight_ref, *refs):
    got_refs, part_refs = refs[: n - 1], refs[n - 1 : 2 * n - 2]
    grad_ref, key_ref, val_ref, slope_ref = refs[2 * n - 2 :]
    scale = HEAD ** (-0.5)
    for h in range(heads):
        total = own_ref[head_cols(h), :]
        for ref in got_refs:
            total = total + read_message(ref, h, heads)
        grad_ref[0, :, head_cols(h)] = (scale * total).T.astype(BF16)
    piece = weight_ref.shape[0] - 8
    width = weight_ref.shape[1] // 2
    total = weight_ref[:piece, :]
    slopes = weight_ref[piece:, :]
    place = lax.broadcasted_iota(jnp.int32, slopes.shape, 0)
    for ref in part_refs:
        extra = ref[piece:, :].astype(jnp.int32).astype(F32)
        total = total + ref[:piece, :].astype(jnp.int32).astype(F32) * (jnp.exp2(extra[0:1, :]) * (1.0 / CODE_MAX))
        for h in range(heads):
            exponent, steps, left = (extra[1 + 3 * h + i : 2 + 3 * h + i, :] for i in range(3))
            value = (steps + left * (1.0 / CODE_MAX)) * (jnp.exp2(exponent) * (1.0 / CODE_MAX))
            slopes = jnp.where(place == h, slopes + value, slopes)
    key_ref[...] = total[:, :width]
    val_ref[...] = total[:, width:]
    slope_ref[...] = slopes[:, :128]


def call(kernel, name, outs, args, scratch=(), smem=0, limit=40 << 20):
    return pl.pallas_call(
        kernel,
        out_shape=[jax.ShapeDtypeStruct(shape, dtype) for shape, dtype in outs],
        in_specs=[SMEM] * smem + [VMEM] * (len(args) - smem),
        out_specs=[VMEM] * len(outs),
        scratch_shapes=list(scratch),
        compiler_params=pltpu.CompilerParams(vmem_limit_bytes=limit),
        name=name,
    )(*args)


def per_device_blocks(n, tokens, levels, boundaries, level_table, w_key, w_value, slopes, queries, cotangent):
    toks, channels = tokens.shape[1:]
    rows, width = queries.shape[1:]
    heads = width // HEAD
    lats = n * rows
    peers = range(1, n)
    q_all = [queries] + [swap(queries, "seq", k, n) for k in peers]
    inputs, keys, values = call(
        prep_kernel,
        "prep",
        [((toks, channels), BF16), ((toks, width), BF16), ((toks, width), BF16)],
        (tokens, levels, level_table, w_key, w_value),
    )
    g_all = [cotangent] + [swap(cotangent, "seq", k, n) for k in peers]
    episode = pltpu.VMEM((toks, 128), F32)
    stat_rows = -(-(heads * n + 1) // 8) * 8
    (top_own,) = call(
        functools.partial(top_kernel, n),
        "tops",
        [((stat_rows, rows), F32)],
        (boundaries, slopes, keys, *q_all),
        [episode],
        2,
    )
    tops = [top_own] + [swap(top_own, "seq", k, n) for k in peers]
    message = ((heads * HEAD + 16 * heads, rows), I16)
    blocks = pltpu.VMEM((lats, width), BF16)
    sums = call(
        functools.partial(sums_kernel, n),
        "sums",
        [((2 * heads * n, rows), F32), ((width, rows), F32)] + [message] * (n - 1),
        (boundaries, slopes, keys, values, *q_all, *g_all, *tops),
        [episode, blocks, blocks, pltpu.VMEM((HEAD, lats), F32)],
        2,
    )
    norms = [sums[0]] + [swap(sums[0], "seq", k, n) for k in peers]
    outs = [swap(sums[1 + k], "seq", k, n) for k in peers]
    half = channels // 2
    grads = call(
        functools.partial(grads_kernel, n),
        "grads",
        [((width, rows), F32)] + [((half + 8, 2 * width), F32)] * 2 + [message] * (n - 1),
        (boundaries, slopes, inputs, keys, values, *q_all, *g_all, *tops, *norms),
        [
            episode,
            blocks,
            blocks,
            pltpu.VMEM((HEAD, lats), F32),
            pltpu.VMEM((toks, 2 * width), BF16),
            pltpu.VMEM((2, half, 2 * width), F32),
        ],
        2,
    )
    got = swap(grads[2], "dp", 1, 2)
    dqs = [swap(grads[2 + k], "seq", k, n) for k in peers]
    (attended,) = call(
        functools.partial(attended_kernel, n, heads),
        "attended",
        [((1, rows, width), BF16)],
        (sums[1], *outs, *norms),
    )
    piece = half // n
    pair = call(
        functools.partial(pair_kernel, n, heads),
        "pair",
        [((piece + 8, 2 * width), F32)] + [((piece + 16, 2 * width), I16)] * (n - 1),
        (grads[1], got),
    )
    parts = [swap(pair[k], "seq", k, n) for k in peers]
    query_grad, key_grad, value_grad, slope_grad = call(
        functools.partial(last_kernel, n, heads),
        "last",
        [((1, rows, width), BF16), ((piece, width), F32), ((piece, width), F32), ((8, 128), F32)],
        (grads[0], pair[0], *dqs, *parts),
    )
    return attended, query_grad, key_grad, value_grad, slope_grad[:heads, 0]


def carried_in(part, axis, combine, identity):
    place = lax.axis_index(axis)
    gathered = lax.all_gather(part, axis)
    state = jnp.zeros_like(part) + jnp.asarray(identity, part.dtype)

    def one(step, state):
        return combine(state, lax.dynamic_index_in_dim(gathered, step, 0, False))

    return lax.fori_loop(0, place, one, state)


def add_counts(earlier, later):
    return earlier + later


def per_device_general(tokens, levels, boundaries, level_table, w_key, w_value, slopes, queries, cotangent):
    scale = HEAD ** (-0.5)
    raw = tokens[0].astype(jnp.float32)
    centered = raw - jnp.mean(raw, axis=1, keepdims=True)
    normed = centered / jnp.sqrt(jnp.mean(centered * centered, axis=1, keepdims=True) + 1e-05)
    lookup = jnp.take(level_table, levels[0], axis=0)
    inputs = (normed + lookup).astype(jnp.bfloat16)
    keys = jnp.dot(inputs, w_key, preferred_element_type=jnp.float32).astype(jnp.bfloat16)
    values = jnp.dot(inputs, w_value, preferred_element_type=jnp.float32).astype(jnp.bfloat16)
    bounds = boundaries[0]
    has = (bounds < BLOCK).astype(jnp.int32)
    earlier = carried_in(jnp.sum(has).reshape(1), "seq", add_counts, jnp.zeros((1,), jnp.int32))
    before = earlier[0] + jnp.cumsum(has) - has
    position = jnp.arange(BLOCK, dtype=jnp.int32)
    inside = (position[None, :] >= bounds[:, None]).astype(jnp.int32)
    episode = (before[:, None] + inside).reshape(-1).astype(jnp.float32)
    query_all, grad_all = (
        lax.all_gather(queries[0], "seq", axis=0, tiled=True),
        lax.all_gather(cotangent[0], "seq", axis=0, tiled=True),
    )
    latents = query_all.shape[0]
    heads = w_key.shape[1] // HEAD
    tok_rows = keys.shape[0]
    own_rows = queries.shape[1]
    start = lax.axis_index("seq") * own_rows
    query_heads = query_all.reshape(latents, heads, HEAD)
    grad_heads = grad_all.reshape(latents, heads, HEAD)
    key_heads = keys.reshape(tok_rows, heads, HEAD)
    value_heads = values.reshape(tok_rows, heads, HEAD)
    score = (
        jnp.einsum("nhd,thd->hnt", query_heads, key_heads, preferred_element_type=jnp.float32)
        * scale
    )
    score = score + slopes[:, None, None] * episode[None, None, :]
    top = lax.pmax(jnp.max(score, axis=2), "seq")
    expo = jnp.exp(score - top[:, :, None])
    part_norm = jnp.sum(expo, axis=2)
    part_out = jnp.einsum(
        "hnt,thd->nhd", expo.astype(jnp.bfloat16), value_heads, preferred_element_type=jnp.float32
    ).reshape(latents, heads * HEAD)
    grad_f32 = grad_all.astype(jnp.float32)
    summed, total = lax.psum((part_out, part_norm), "seq")
    mixed = (summed.reshape(latents, heads, HEAD) / total.T[:, :, None]).reshape(
        latents, heads * HEAD
    )
    delta = jnp.sum((grad_f32 * mixed).reshape(latents, heads, HEAD), axis=2).T
    own_mixed = lax.dynamic_slice_in_dim(mixed, start, own_rows, 0)
    attended = own_mixed.astype(jnp.bfloat16)[None]
    probs = expo / total[:, :, None]
    probs_b = probs.astype(jnp.bfloat16)
    value_tok = (
        jnp.einsum("hnt,nhd->thd", probs_b, grad_heads, preferred_element_type=jnp.float32)
        .astype(jnp.bfloat16)
        .reshape(tok_rows, heads * HEAD)
    )
    dprod = jnp.einsum("nhd,thd->hnt", grad_heads, value_heads, preferred_element_type=jnp.float32)
    score_grad = probs * (dprod - delta[:, :, None])
    slope_part = jnp.sum(score_grad * episode[None, None, :], axis=(1, 2))
    score_grad_b = score_grad.astype(jnp.bfloat16)
    query_part = (
        scale
        * jnp.einsum("hnt,thd->nhd", score_grad_b, key_heads, preferred_element_type=jnp.float32)
    ).reshape(latents, heads * HEAD)
    key_tok = (
        (
            scale
            * jnp.einsum(
                "hnt,nhd->thd", score_grad_b, query_heads, preferred_element_type=jnp.float32
            )
        )
        .astype(jnp.bfloat16)
        .reshape(tok_rows, heads * HEAD)
    )
    query_grad = lax.psum_scatter(query_part, "seq", scatter_dimension=0, tiled=True).astype(
        jnp.bfloat16
    )[None]
    key_part = jnp.dot(inputs.T, key_tok, preferred_element_type=jnp.float32)
    value_part = jnp.dot(inputs.T, value_tok, preferred_element_type=jnp.float32)
    key_weight_grad, value_weight_grad = (
        lax.psum_scatter(key_part, ("dp", "seq"), scatter_dimension=0, tiled=True),
        lax.psum_scatter(value_part, ("dp", "seq"), scatter_dimension=0, tiled=True),
    )
    slope_grad = lax.psum(slope_part, ("dp", "seq"))
    return (attended, query_grad, key_weight_grad, value_weight_grad, slope_grad)


def solution(mesh):
    n = mesh.shape["seq"]

    def per_device(*args):
        rows = args[7].shape[1]
        if n in (2, 4, 8) and mesh.shape["dp"] == 2 and rows % 128 == 0:
            return per_device_blocks(n, *args)
        return per_device_general(*args)

    return jax.shard_map(
        per_device,
        mesh=mesh,
        in_specs=(
            P("dp", "seq", None),
            P("dp", "seq"),
            P("dp", "seq"),
            P(),
            P(None, "tensor"),
            P(None, "tensor"),
            P("tensor"),
            P("dp", "seq", "tensor"),
            P("dp", "seq", "tensor"),
        ),
        out_specs=(
            P("dp", "seq", "tensor"),
            P("dp", "seq", "tensor"),
            P(("dp", "seq"), "tensor"),
            P(("dp", "seq"), "tensor"),
            P("tensor"),
        ),
        check_vma=False,
    )
```

```python
import functools

import jax
import jax.numpy as jnp
from jax import lax
from jax.experimental import pallas as pl
from jax.experimental.pallas import tpu as pltpu
from jax.sharding import PartitionSpec as P

HEAD = 128
BLOCK = 128
LOG2E = 1.4426950408889634
CODE_MAX = 32000.0
TINY = 1e-30
CHUNK = 256
STEP = 512
LIM_P, LIM_T, LIM_D, LIM_S, LIM_G = 55, 8, 8, 16, 16
SCALE = HEAD ** (-0.5)
UNIT = SCALE * LOG2E

F32 = jnp.float32
BF16 = jnp.bfloat16
I16 = jnp.int16
VMEM = pl.BlockSpec(memory_space=pltpu.VMEM)
SMEM = pl.BlockSpec(memory_space=pltpu.SMEM)


def nn(a, b):
    return lax.dot_general(a, b, (((1,), (0,)), ((), ())), preferred_element_type=F32)


def nt(a, b):
    return lax.dot_general(a, b, (((1,), (1,)), ((), ())), preferred_element_type=F32)


def tn(a, b):
    return lax.dot_general(a, b, (((0,), (0,)), ((), ())), preferred_element_type=F32)


def head_cols(h):
    return slice(h * HEAD, (h + 1) * HEAD)


def swap(x, axis, k, n):
    return lax.ppermute(x, axis, [(i, i ^ k) for i in range(n)])


def encode(x):
    most = jnp.maximum(jnp.max(jnp.abs(x), axis=0, keepdims=True), TINY)
    exponent = jnp.ceil(jnp.log2(most))
    steps = jnp.round(x * (jnp.exp2(-exponent) * CODE_MAX))
    return steps, exponent


def decode(steps, exponent):
    return steps.astype(jnp.int32).astype(F32) * (jnp.exp2(exponent.astype(jnp.int32).astype(F32)) * (1.0 / CODE_MAX))


def to_code(x):
    return x.astype(jnp.int32).astype(I16)


def stack_rows(rows, total, width):
    place = lax.broadcasted_iota(jnp.int32, (total, width), 0)
    out = jnp.zeros((total, width), F32)
    for i, row in enumerate(rows):
        out = jnp.where(place == i, row, out)
    return out


def prep_kernel(tok_hbm, lev_hbm, table_hbm, wk_hbm, wv_hbm, g_hbm, inp_ref, key_ref, val_ref, g_ref, *scratch):
    tok_ref, lev_ref, table_ref, wk_ref, wv_ref, sems = scratch
    first = [(table_hbm, table_ref), (lev_hbm, lev_ref), (wk_hbm, wk_ref), (wv_hbm, wv_ref), (g_hbm, g_ref)]
    parts = [slice(c * CHUNK, (c + 1) * CHUNK) for c in range(tok_ref.shape[1] // CHUNK)]
    pairs = first + [(tok_hbm.at[:, part, :], tok_ref.at[:, part, :]) for part in parts]
    copies = [pltpu.make_async_copy(src, dst, sems.at[i]) for i, (src, dst) in enumerate(pairs)]
    for copy in copies:
        copy.start()
    for copy in copies[: len(first)]:
        copy.wait()
    table = table_ref[...]
    hi = table.astype(BF16)
    rest = table - hi.astype(F32)
    mid = rest.astype(BF16)
    low = (rest - mid.astype(F32)).astype(BF16)
    levels = table.shape[0]
    for c, rows in enumerate(parts):
        copies[len(first) + c].wait()
        raw = tok_ref[0, rows, :].astype(F32)
        centered = raw - jnp.mean(raw, axis=1, keepdims=True)
        normed = centered / jnp.sqrt(jnp.mean(centered * centered, axis=1, keepdims=True) + 1e-05)
        ids = lev_ref[0:1, rows]
        pick = (lax.broadcasted_iota(jnp.int32, (levels, CHUNK), 0) == ids).astype(F32).astype(BF16)
        lookup = (tn(pick, low) + tn(pick, mid)) + tn(pick, hi)
        inputs = (normed + lookup).astype(BF16)
        inp_ref[rows, :] = inputs
        key_ref[rows, :] = nn(inputs, wk_ref[...]).astype(BF16)
        val_ref[rows, :] = nn(inputs, wv_ref[...]).astype(BF16)


def three(x):
    hi = x.astype(BF16).astype(F32)
    mid = (x - hi).astype(BF16).astype(F32)
    return [hi, mid, x - hi - mid]


def fill_episode(bounds_ref, episode_ref, base):
    before = jnp.int32(0)
    shape = (BLOCK, episode_ref.shape[1])
    place = lax.broadcasted_iota(jnp.int32, shape, 0)
    for b in range(bounds_ref.shape[1]):
        bound = bounds_ref[0, b]
        episode = base + (before + (place >= bound).astype(jnp.int32)).astype(F32)
        episode_ref[b * BLOCK : (b + 1) * BLOCK, :] = episode.astype(episode_ref.dtype)
        before = before + (bound < BLOCK).astype(jnp.int32)
    return before


def slope_of(slopes_ref, h, width):
    return jnp.full((1, width), slopes_ref[h] * (1.0 / SCALE), F32)


def top_kernel(n, bounds_ref, slopes_ref, key_ref, *refs):
    q_refs, (stats_ref, score_ref, side_ref) = refs[:n], refs[n:]
    rows = q_refs[0].shape[1]
    tokens, width = key_ref.shape
    heads = width // HEAD
    starts = fill_episode(bounds_ref, side_ref, 0.0)
    lane = lax.broadcasted_iota(jnp.int32, (rows, 128), 1)
    for h in range(heads):
        beside = jnp.zeros((rows, 128), F32)
        for i, term in enumerate(three(slope_of(slopes_ref, h, 128))):
            beside = jnp.where(lane == i, term, beside)
        beside = beside.astype(BF16)
        keys = jnp.concatenate([key_ref[:, head_cols(h)], side_ref[...]], axis=1)
        for j in range(n):
            query = jnp.concatenate([q_refs[j][0, :, head_cols(h)], beside], axis=1)
            score = nt(keys, query)
            score_ref[h, :, j * rows : (j + 1) * rows] = score
            stats_ref[h * n + j : h * n + j + 1, :] = jnp.max(score, axis=0, keepdims=True)
    stats_ref[heads * n : heads * n + 1, :] = jnp.zeros((1, rows), F32) + starts.astype(F32)


def dprod_kernel(n, val_ref, *refs):
    q_refs, g_refs, (dprod_ref, qt_ref, gt_ref) = refs[:n], refs[n : 2 * n], refs[2 * n :]
    rows = q_refs[0].shape[1]
    for j in range(n):
        cols = slice(j * rows, (j + 1) * rows)
        qt_ref[:, cols] = q_refs[j][0].astype(F32).T.astype(BF16)
        gt_ref[:, cols] = g_refs[j][0].astype(F32).T.astype(BF16)
        for h in range(dprod_ref.shape[0]):
            dprod_ref[h, :, cols] = nt(val_ref[:, head_cols(h)], g_refs[j][0, :, head_cols(h)])


def merged_tops(n, heads, slopes_ref, stats_refs):
    me = lax.axis_index("seq")
    counts = [ref[heads * n : heads * n + 1, :] for ref in stats_refs]
    bases = []
    for k in range(n):
        base = jnp.zeros_like(counts[0])
        for j in range(n):
            earlier = ((me ^ j) < (me ^ k)).astype(F32)
            base = base + earlier * counts[j]
        bases.append(base)
    tops = []
    for h in range(heads):
        row = []
        for j in range(n):
            best = None
            for k in range(n):
                place = h * n + (j ^ k)
                top = stats_refs[k][place : place + 1, :] + slope_of(slopes_ref, h, bases[k].shape[1]) * bases[k]
                best = top if best is None else jnp.maximum(best, top)
            row.append(best)
        tops.append(row)
    return tops, bases[0]


def sums_kernel(n, slopes_ref, val_ref, score_ref, gt_ref, *refs):
    top_refs, (stats_ref, own_ref, expo_ref) = refs[:n], refs[n : n + 3]
    send_refs = refs[n + 3 : 2 * n + 2]
    (out_ref,) = refs[2 * n + 2 :]
    heads, tokens, lats = score_ref.shape
    rows = lats // n
    tops, base = merged_tops(n, heads, slopes_ref, top_refs)
    for h in range(heads):
        slope = slope_of(slopes_ref, h, rows)
        top = jnp.concatenate([t - slope * base for t in tops[h]], axis=1)
        norm = out = None
        for c in range(tokens // STEP):
            part = slice(c * STEP, (c + 1) * STEP)
            expo = jnp.exp2((score_ref[h, part, :] - top) * UNIT)
            expo_ref[h, part, :] = expo
            term = tn(val_ref[part, head_cols(h)], expo.astype(BF16))
            part_norm = jnp.sum(expo, axis=0, keepdims=True)
            out = term if out is None else out + term
            norm = part_norm if norm is None else norm + part_norm
        out_ref[...] = out
        delta = jnp.sum(gt_ref[head_cols(h), :].astype(F32) * out, axis=0, keepdims=True)
        for j in range(n):
            cols = slice(j * rows, (j + 1) * rows)
            stats_ref[h * n + j : h * n + j + 1, :] = norm[:, cols]
            place = heads * n + h * n + j
            stats_ref[place : place + 1, :] = delta[:, cols]
        own_ref[head_cols(h), :] = out_ref[:, :rows]
        write_messages(h, n, rows, heads, out_ref, send_refs)


def write_messages(h, n, rows, heads, sums_ref, send_refs):
    for j in range(1, n):
        steps, exponent = encode(sums_ref[:, j * rows : (j + 1) * rows])
        send_refs[j - 1][head_cols(h), :] = to_code(steps)
        place = heads * HEAD + h * 16
        send_refs[j - 1][place : place + 16, :] = to_code(jnp.broadcast_to(exponent, (16, rows)))


def read_message(ref, h, heads):
    place = heads * HEAD + h * 16
    return decode(ref[head_cols(h), :], ref[place : place + 16, :][0:1, :])


def merged_sums(n, heads, stats_refs):
    norms, deltas = [], []
    for h in range(heads):
        norm_row, delta_row = [], []
        for j in range(n):
            norm = delta = None
            for k in range(n):
                place = h * n + (j ^ k)
                a = stats_refs[k][place : place + 1, :]
                b = stats_refs[k][heads * n + place : heads * n + place + 1, :]
                norm = a if norm is None else norm + a
                delta = b if delta is None else delta + b
            norm_row.append(norm)
            delta_row.append(delta)
        norms.append(jnp.concatenate(norm_row, axis=1))
        deltas.append(jnp.concatenate(delta_row, axis=1))
    return norms, deltas


def grads_kernel(n, h, heads, bounds_ref, slopes_ref, inp_ref, key_ref, expo_ref, dprod_ref, qt_ref, gt_ref, *refs):
    top_refs, sum_refs, refs = refs[:n], refs[n : 2 * n], refs[2 * n :]
    outs = n + 2
    old, _, refs = (refs[:outs], refs[outs], refs[outs + 1 :]) if h else (None, None, refs)
    own_ref, keep_ref, give_ref = refs[:3]
    send_refs = refs[3:outs]
    episode_ref, dq_ref, tok_ref, weight_ref = refs[outs:]
    _, tokens, lats = expo_ref.shape
    _, base = merged_tops(n, heads, slopes_ref, top_refs)
    norms, deltas = merged_sums(n, heads, sum_refs)
    fill_episode(bounds_ref, episode_ref, base[:, :128])
    inverse = 1.0 / norms[h]
    mean = deltas[h] * inverse
    slope = jnp.zeros((1, 128), F32)
    dq = None
    for c in range(tokens // STEP):
        part = slice(c * STEP, (c + 1) * STEP)
        probs = expo_ref[h, part, :] * inverse
        tok_ref[HEAD:, part] = nt(gt_ref[head_cols(h), :], probs.astype(BF16)).astype(BF16)
        score_grad = probs * (dprod_ref[h, part, :] - mean)
        folded = score_grad[:, :128]
        for i in range(1, lats // 128):
            folded = folded + score_grad[:, i * 128 : (i + 1) * 128]
        slope = slope + jnp.sum(folded * episode_ref[part, :], axis=0, keepdims=True)
        score_grad_b = score_grad.astype(BF16)
        tok_ref[:HEAD, part] = (SCALE * nt(qt_ref[head_cols(h), :], score_grad_b)).astype(BF16)
        term = tn(key_ref[part, head_cols(h)], score_grad_b)
        dq = term if dq is None else dq + term
    dq_ref[...] = dq
    if h:
        done, cols = h * HEAD, h * 2 * HEAD
        own_ref[:done, :] = old[0][:done, :]
        keep_ref[:, :cols] = old[1][:, :cols]
        give_ref[:, :cols] = old[2][:, :cols]
        for ref, was in zip(send_refs, old[3:]):
            ref[:done, :] = was[:done, :]
            ref[heads * HEAD : heads * HEAD + 16 * h, :] = was[heads * HEAD : heads * HEAD + 16 * h, :]
    rows = lats // n
    own_ref[head_cols(h), :] = dq_ref[:, :rows]
    write_messages(h, n, rows, heads, dq_ref, send_refs)
    half = keep_ref.shape[0] - 8
    for i in range(2):
        side = inp_ref[:, i * half : (i + 1) * half]
        weight_ref[i] = lax.dot_general(side, tok_ref[...], (((0,), (1,)), ((), ())), preferred_element_type=F32)
    core = lax.axis_index("dp")
    cols = slice(h * 2 * HEAD, (h + 1) * 2 * HEAD)
    total = jnp.broadcast_to(jnp.sum(slope, axis=1, keepdims=True), (8, 2 * HEAD))
    keep_ref[:half, cols] = weight_ref[core]
    give_ref[:half, cols] = weight_ref[1 - core]
    keep_ref[half:, cols] = total
    give_ref[half:, cols] = total


def pair_kernel(n, heads, keep_ref, got_ref, own_ref, *send_refs):
    me = lax.axis_index("seq")
    half = keep_ref.shape[0] - 8
    piece = half // n
    width = keep_ref.shape[1]
    slopes = keep_ref[half:, :] + got_ref[half:, :]
    value = slopes[0:1, :]
    steps, exponent = encode(value)
    left = value * (jnp.exp2(-exponent) * CODE_MAX) - steps
    digits = [exponent, steps, jnp.round(left * CODE_MAX)]
    for k in range(n):
        rows = pl.ds(pl.multiple_of((me ^ k) * piece, piece), piece)
        total = keep_ref[rows, :] + got_ref[rows, :]
        if k == 0:
            own_ref[:piece, :] = total
            own_ref[piece:, :] = slopes
        else:
            steps, exponent = encode(total)
            send_refs[k - 1][:piece, :] = to_code(steps)
            send_refs[k - 1][piece:, :] = to_code(stack_rows([exponent] + digits, 16, width))


def attended_kernel(n, heads, own_ref, *refs):
    got_refs, sum_refs, out_ref = refs[: n - 1], refs[n - 1 : 2 * n - 1], refs[2 * n - 1]
    refs[2 * n][...] = jnp.zeros_like(refs[2 * n])
    rows = own_ref.shape[1]
    norms, _ = merged_sums(n, heads, sum_refs)
    for h in range(heads):
        total = own_ref[head_cols(h), :]
        for ref in got_refs:
            total = total + read_message(ref, h, heads)
        total = total / norms[h][:, :rows]
        out_ref[0, :, head_cols(h)] = total.T.astype(BF16)


def last_kernel(n, heads, own_ref, weight_ref, *refs):
    got_refs, part_refs = refs[: n - 1], refs[n - 1 : 2 * n - 2]
    grad_ref, key_ref, val_ref, slope_ref = refs[2 * n - 2 :]
    for h in range(heads):
        total = own_ref[head_cols(h), :]
        for ref in got_refs:
            total = total + read_message(ref, h, heads)
        grad_ref[0, :, head_cols(h)] = (SCALE * total).T.astype(BF16)
    piece = weight_ref.shape[0] - 8
    total = weight_ref[:piece, :]
    slopes = weight_ref[piece : piece + 1, :]
    for ref in part_refs:
        extra = ref[piece:, :].astype(jnp.int32).astype(F32)
        total = total + ref[:piece, :].astype(jnp.int32).astype(F32) * (jnp.exp2(extra[0:1, :]) * (1.0 / CODE_MAX))
        exponent, steps, left = (extra[i : i + 1, :] for i in range(1, 4))
        slopes = slopes + (steps + left * (1.0 / CODE_MAX)) * (jnp.exp2(exponent) * (1.0 / CODE_MAX))
    for h in range(heads):
        at = h * 2 * HEAD
        key_ref[:, head_cols(h)] = total[:, at : at + HEAD]
        val_ref[:, head_cols(h)] = total[:, at + HEAD : at + 2 * HEAD]
        slope_ref[h] = slopes[0, at]


def call(kernel, name, outs, args, us, scratch=(), smem=0, limit=8 << 20, ins=None, out_specs=None):
    return pl.pallas_call(
        kernel,
        out_shape=[jax.ShapeDtypeStruct(shape, dtype) for shape, dtype in outs],
        in_specs=ins or [SMEM] * smem + [VMEM] * (len(args) - smem),
        out_specs=out_specs or [VMEM] * len(outs),
        scratch_shapes=list(scratch),
        compiler_params=pltpu.CompilerParams(vmem_limit_bytes=limit),
        cost_estimate=pl.CostEstimate(flops=int(us * 1.1e9), bytes_accessed=1 << 16, transcendentals=0),
        name=name,
    )(*args)


def per_device_blocks(n, tokens, levels, boundaries, level_table, w_key, w_value, slopes, queries, cotangent):
    toks, channels = tokens.shape[1:]
    rows, width = queries.shape[1:]
    heads = width // HEAD
    lats = n * rows
    peers = range(1, n)
    q_all = [queries] + [swap(queries, "seq", k, n) for k in peers]
    prep_args = (tokens, levels, level_table, w_key, w_value)
    inputs, keys, values, grad = call(
        prep_kernel,
        "prep",
        [((toks, channels), BF16), ((toks, width), BF16), ((toks, width), BF16), (cotangent.shape, BF16)],
        (*prep_args, cotangent),
        3,
        [pltpu.VMEM(a.shape, a.dtype) for a in prep_args] + [pltpu.SemaphoreType.DMA((5 + toks // CHUNK,))],
        limit=LIM_P << 20,
        ins=[pl.BlockSpec(memory_space=pltpu.HBM)] * 6,
    )
    g_all = [grad] + [swap(grad, "seq", k, n) for k in peers]
    stat_rows = -(-(heads * n + 1) // 8) * 8
    square = ((heads, toks, lats), F32)
    top_own, scores = call(
        functools.partial(top_kernel, n),
        "tops",
        [((stat_rows, rows), F32), square],
        (boundaries, slopes, keys, *q_all),
        2,
        [pltpu.VMEM((toks, 128), BF16)],
        2,
        limit=LIM_T << 20,
    )
    tops = [top_own] + [swap(top_own, "seq", k, n) for k in peers]
    dprod, q_turned, g_turned = call(
        functools.partial(dprod_kernel, n),
        "dprod",
        [square, ((width, lats), BF16), ((width, lats), BF16)],
        (values, *q_all, *g_all),
        2,
        limit=LIM_D << 20,
    )
    message = ((heads * HEAD + 16 * heads, rows), I16)
    partial = pltpu.VMEM((HEAD, lats), F32)
    sums = call(
        functools.partial(sums_kernel, n),
        "sums",
        [((2 * heads * n, rows), F32), ((width, rows), F32), square] + [message] * (n - 1),
        (slopes, values, scores, g_turned, *tops),
        2,
        [partial],
        1,
        limit=LIM_S << 20,
    )
    norms = [sums[0]] + [swap(sums[0], "seq", k, n) for k in peers]
    outs = [swap(sums[2 + k], "seq", k, n) for k in peers]
    half = channels // 2
    grads = attended = ()
    for h in range(heads):
        grads = call(
            functools.partial(grads_kernel, n, h, heads),
            f"grads{h}",
            [((width, rows), F32)] + [((half + 8, 2 * width), F32)] * 2 + [message] * (n - 1),
            (boundaries, slopes, inputs, keys, sums[2], dprod, q_turned, g_turned, *tops, *norms, *grads, *attended[1:]),
            2,
            [
                pltpu.VMEM((toks, 128), F32),
                partial,
                pltpu.VMEM((2 * HEAD, toks), BF16),
                pltpu.VMEM((2, half, 2 * HEAD), F32),
            ],
            2,
            limit=LIM_G << 20,
        )
        if h == 0:
            attended = call(
                functools.partial(attended_kernel, n, heads),
                "attended",
                [((1, rows, width), BF16), ((8, 128), F32)],
                (sums[1], *outs, *norms),
                1,
            )
    got = swap(grads[2], "dp", 1, 2)
    dqs = [swap(grads[2 + k], "seq", k, n) for k in peers]
    piece = half // n
    pair = call(
        functools.partial(pair_kernel, n, heads),
        "pair",
        [((piece + 8, 2 * width), F32)] + [((piece + 16, 2 * width), I16)] * (n - 1),
        (grads[1], got),
        0.3,
    )
    parts = [swap(pair[k], "seq", k, n) for k in peers]
    last = call(
        functools.partial(last_kernel, n, heads),
        "last",
        [((1, rows, width), BF16), ((piece, width), F32), ((piece, width), F32), ((heads,), F32)],
        (grads[0], pair[0], *dqs, *parts),
        1,
        out_specs=[VMEM] * 3 + [SMEM],
    )
    return (attended[0], *last)


def carried_in(part, axis, combine, identity):
    place = lax.axis_index(axis)
    gathered = lax.all_gather(part, axis)
    state = jnp.zeros_like(part) + jnp.asarray(identity, part.dtype)

    def one(step, state):
        return combine(state, lax.dynamic_index_in_dim(gathered, step, 0, False))

    return lax.fori_loop(0, place, one, state)


def add_counts(earlier, later):
    return earlier + later


def per_device_general(tokens, levels, boundaries, level_table, w_key, w_value, slopes, queries, cotangent):
    scale = HEAD ** (-0.5)
    raw = tokens[0].astype(jnp.float32)
    centered = raw - jnp.mean(raw, axis=1, keepdims=True)
    normed = centered / jnp.sqrt(jnp.mean(centered * centered, axis=1, keepdims=True) + 1e-05)
    lookup = jnp.take(level_table, levels[0], axis=0)
    inputs = (normed + lookup).astype(jnp.bfloat16)
    keys = jnp.dot(inputs, w_key, preferred_element_type=jnp.float32).astype(jnp.bfloat16)
    values = jnp.dot(inputs, w_value, preferred_element_type=jnp.float32).astype(jnp.bfloat16)
    bounds = boundaries[0]
    has = (bounds < BLOCK).astype(jnp.int32)
    earlier = carried_in(jnp.sum(has).reshape(1), "seq", add_counts, jnp.zeros((1,), jnp.int32))
    before = earlier[0] + jnp.cumsum(has) - has
    position = jnp.arange(BLOCK, dtype=jnp.int32)
    inside = (position[None, :] >= bounds[:, None]).astype(jnp.int32)
    episode = (before[:, None] + inside).reshape(-1).astype(jnp.float32)
    query_all, grad_all = (
        lax.all_gather(queries[0], "seq", axis=0, tiled=True),
        lax.all_gather(cotangent[0], "seq", axis=0, tiled=True),
    )
    latents = query_all.shape[0]
    heads = w_key.shape[1] // HEAD
    tok_rows = keys.shape[0]
    own_rows = queries.shape[1]
    start = lax.axis_index("seq") * own_rows
    query_heads = query_all.reshape(latents, heads, HEAD)
    grad_heads = grad_all.reshape(latents, heads, HEAD)
    key_heads = keys.reshape(tok_rows, heads, HEAD)
    value_heads = values.reshape(tok_rows, heads, HEAD)
    score = (
        jnp.einsum("nhd,thd->hnt", query_heads, key_heads, preferred_element_type=jnp.float32)
        * scale
    )
    score = score + slopes[:, None, None] * episode[None, None, :]
    top = lax.pmax(jnp.max(score, axis=2), "seq")
    expo = jnp.exp(score - top[:, :, None])
    part_norm = jnp.sum(expo, axis=2)
    part_out = jnp.einsum(
        "hnt,thd->nhd", expo.astype(jnp.bfloat16), value_heads, preferred_element_type=jnp.float32
    ).reshape(latents, heads * HEAD)
    grad_f32 = grad_all.astype(jnp.float32)
    summed, total = lax.psum((part_out, part_norm), "seq")
    mixed = (summed.reshape(latents, heads, HEAD) / total.T[:, :, None]).reshape(
        latents, heads * HEAD
    )
    delta = jnp.sum((grad_f32 * mixed).reshape(latents, heads, HEAD), axis=2).T
    own_mixed = lax.dynamic_slice_in_dim(mixed, start, own_rows, 0)
    attended = own_mixed.astype(jnp.bfloat16)[None]
    probs = expo / total[:, :, None]
    probs_b = probs.astype(jnp.bfloat16)
    value_tok = (
        jnp.einsum("hnt,nhd->thd", probs_b, grad_heads, preferred_element_type=jnp.float32)
        .astype(jnp.bfloat16)
        .reshape(tok_rows, heads * HEAD)
    )
    dprod = jnp.einsum("nhd,thd->hnt", grad_heads, value_heads, preferred_element_type=jnp.float32)
    score_grad = probs * (dprod - delta[:, :, None])
    slope_part = jnp.sum(score_grad * episode[None, None, :], axis=(1, 2))
    score_grad_b = score_grad.astype(jnp.bfloat16)
    query_part = (
        scale
        * jnp.einsum("hnt,thd->nhd", score_grad_b, key_heads, preferred_element_type=jnp.float32)
    ).reshape(latents, heads * HEAD)
    key_tok = (
        (
            scale
            * jnp.einsum(
                "hnt,nhd->thd", score_grad_b, query_heads, preferred_element_type=jnp.float32
            )
        )
        .astype(jnp.bfloat16)
        .reshape(tok_rows, heads * HEAD)
    )
    query_grad = lax.psum_scatter(query_part, "seq", scatter_dimension=0, tiled=True).astype(
        jnp.bfloat16
    )[None]
    key_part = jnp.dot(inputs.T, key_tok, preferred_element_type=jnp.float32)
    value_part = jnp.dot(inputs.T, value_tok, preferred_element_type=jnp.float32)
    key_weight_grad, value_weight_grad = (
        lax.psum_scatter(key_part, ("dp", "seq"), scatter_dimension=0, tiled=True),
        lax.psum_scatter(value_part, ("dp", "seq"), scatter_dimension=0, tiled=True),
    )
    slope_grad = lax.psum(slope_part, ("dp", "seq"))
    return (attended, query_grad, key_weight_grad, value_weight_grad, slope_grad)


def solution(mesh):
    n = mesh.shape["seq"]

    def per_device(*args):
        rows = args[7].shape[1]
        if n in (2, 4, 8) and mesh.shape["dp"] == 2 and rows % 128 == 0:
            return per_device_blocks(n, *args)
        return per_device_general(*args)

    return jax.shard_map(
        per_device,
        mesh=mesh,
        in_specs=(
            P("dp", "seq", None),
            P("dp", "seq"),
            P("dp", "seq"),
            P(),
            P(None, "tensor"),
            P(None, "tensor"),
            P("tensor"),
            P("dp", "seq", "tensor"),
            P("dp", "seq", "tensor"),
        ),
        out_specs=(
            P("dp", "seq", "tensor"),
            P("dp", "seq", "tensor"),
            P(("dp", "seq"), "tensor"),
            P(("dp", "seq"), "tensor"),
            P("tensor"),
        ),
        check_vma=False,
    )
```

```python
import functools

import jax
import jax.numpy as jnp
from jax import lax
from jax.experimental import pallas as pl
from jax.experimental.pallas import tpu as pltpu
from jax.sharding import PartitionSpec as P

HEAD = 128
BLOCK = 128
LOG2E = 1.4426950408889634
CODE_MAX = 32000.0
TINY = 1e-30
CHUNK = 512
STEP = 512
LIM_P, LIM_T, LIM_D, LIM_S, LIM_G = 55, 8, 8, 16, 16
SCALE = HEAD ** (-0.5)
UNIT = SCALE * LOG2E

F32 = jnp.float32
BF16 = jnp.bfloat16
I16 = jnp.int16
VMEM = pl.BlockSpec(memory_space=pltpu.VMEM)
SMEM = pl.BlockSpec(memory_space=pltpu.SMEM)


def nn(a, b):
    return lax.dot_general(a, b, (((1,), (0,)), ((), ())), preferred_element_type=F32)


def nt(a, b):
    return lax.dot_general(a, b, (((1,), (1,)), ((), ())), preferred_element_type=F32)


def tn(a, b):
    return lax.dot_general(a, b, (((0,), (0,)), ((), ())), preferred_element_type=F32)


def head_cols(h):
    return slice(h * HEAD, (h + 1) * HEAD)


def swap(x, axis, k, n):
    return lax.ppermute(x, axis, [(i, i ^ k) for i in range(n)])


def encode(x):
    most = jnp.maximum(jnp.max(jnp.abs(x), axis=0, keepdims=True), TINY)
    exponent = jnp.ceil(jnp.log2(most))
    steps = jnp.round(x * (jnp.exp2(-exponent) * CODE_MAX))
    return steps, exponent


def decode(steps, exponent):
    return steps * (jnp.exp2(exponent) * (1.0 / CODE_MAX))


def to_code(x):
    return x.astype(jnp.int32).astype(I16)


def from_code(x):
    return x.astype(jnp.int32).astype(F32)


def stack_rows(rows, total, width):
    place = lax.broadcasted_iota(jnp.int32, (total, width), 0)
    out = jnp.zeros((total, width), F32)
    for i, row in enumerate(rows):
        out = jnp.where(place == i, row, out)
    return out


def prep_kernel(tok_hbm, lev_hbm, table_hbm, wk_hbm, wv_hbm, g_hbm, inp_ref, key_ref, val_ref, g_ref, *scratch):
    tok_ref, lev_ref, table_ref, wk_ref, wv_ref, sems = scratch
    first = [(table_hbm, table_ref), (lev_hbm, lev_ref), (wk_hbm, wk_ref), (wv_hbm, wv_ref), (g_hbm, g_ref)]
    parts = [slice(c * CHUNK, (c + 1) * CHUNK) for c in range(tok_ref.shape[1] // CHUNK)]
    pairs = first + [(tok_hbm.at[:, part, :], tok_ref.at[:, part, :]) for part in parts]
    copies = [pltpu.make_async_copy(src, dst, sems.at[i]) for i, (src, dst) in enumerate(pairs)]
    for copy in copies:
        copy.start()
    for copy in copies[: len(first)]:
        copy.wait()
    table = table_ref[...]
    hi = table.astype(BF16)
    rest = table - hi.astype(F32)
    mid = rest.astype(BF16)
    low = (rest - mid.astype(F32)).astype(BF16)
    levels = table.shape[0]
    for c, rows in enumerate(parts):
        copies[len(first) + c].wait()
        raw = tok_ref[0, rows, :].astype(F32)
        centered = raw - jnp.mean(raw, axis=1, keepdims=True)
        normed = centered / jnp.sqrt(jnp.mean(centered * centered, axis=1, keepdims=True) + 1e-05)
        ids = lev_ref[0:1, rows]
        pick = (lax.broadcasted_iota(jnp.int32, (levels, CHUNK), 0) == ids).astype(F32).astype(BF16)
        lookup = (tn(pick, low) + tn(pick, mid)) + tn(pick, hi)
        inputs = (normed + lookup).astype(BF16)
        inp_ref[rows, :] = inputs
        key_ref[rows, :] = nn(inputs, wk_ref[...]).astype(BF16)
        val_ref[rows, :] = nn(inputs, wv_ref[...]).astype(BF16)


def three(x):
    hi = x.astype(BF16).astype(F32)
    mid = (x - hi).astype(BF16).astype(F32)
    return [hi, mid, x - hi - mid]


def fill_episode(bounds_ref, episode_ref, base):
    before = jnp.int32(0)
    shape = (BLOCK, episode_ref.shape[1])
    place = lax.broadcasted_iota(jnp.int32, shape, 0)
    for b in range(bounds_ref.shape[1]):
        bound = bounds_ref[0, b]
        episode = base + (before + (place >= bound).astype(jnp.int32)).astype(F32)
        episode_ref[b * BLOCK : (b + 1) * BLOCK, :] = episode.astype(episode_ref.dtype)
        before = before + (bound < BLOCK).astype(jnp.int32)
    return before


def slope_of(slopes_ref, h, width):
    return jnp.full((1, width), slopes_ref[h] * (1.0 / SCALE), F32)


def top_kernel(n, bounds_ref, slopes_ref, key_ref, *refs):
    q_refs, (stats_ref, score_ref, side_ref) = refs[:n], refs[n:]
    rows = q_refs[0].shape[1]
    tokens, width = key_ref.shape
    heads = width // HEAD
    starts = fill_episode(bounds_ref, side_ref, 0.0)
    lane = lax.broadcasted_iota(jnp.int32, (rows, 128), 1)
    for h in range(heads):
        beside = jnp.zeros((rows, 128), F32)
        for i, term in enumerate(three(slope_of(slopes_ref, h, 128))):
            beside = jnp.where(lane == i, term, beside)
        beside = beside.astype(BF16)
        keys = jnp.concatenate([key_ref[:, head_cols(h)], side_ref[...]], axis=1)
        for j in range(n):
            query = jnp.concatenate([q_refs[j][0, :, head_cols(h)], beside], axis=1)
            score = nt(keys, query)
            score_ref[h, :, j * rows : (j + 1) * rows] = score
            stats_ref[h * n + j : h * n + j + 1, :] = jnp.max(score, axis=0, keepdims=True)
    stats_ref[heads * n : heads * n + 1, :] = jnp.zeros((1, rows), F32) + starts.astype(F32)


def turn_kernel(n, *refs):
    q_refs, g_refs, (qt_ref, gt_ref) = refs[:n], refs[n : 2 * n], refs[2 * n :]
    rows = q_refs[0].shape[1]
    for j in range(n):
        cols = slice(j * rows, (j + 1) * rows)
        qt_ref[:, cols] = q_refs[j][0].astype(F32).T.astype(BF16)
        gt_ref[:, cols] = g_refs[j][0].astype(F32).T.astype(BF16)


def dprod_kernel(val_ref, gt_ref, _, dprod_ref):
    for h in range(dprod_ref.shape[0]):
        dprod_ref[h] = nn(val_ref[:, head_cols(h)], gt_ref[head_cols(h), :])


def merged_tops(n, heads, slopes_ref, stats_refs):
    me = lax.axis_index("seq")
    counts = [ref[heads * n : heads * n + 1, :] for ref in stats_refs]
    bases = []
    for k in range(n):
        base = jnp.zeros_like(counts[0])
        for j in range(n):
            earlier = ((me ^ j) < (me ^ k)).astype(F32)
            base = base + earlier * counts[j]
        bases.append(base)
    tops = []
    for h in range(heads):
        row = []
        for j in range(n):
            best = None
            for k in range(n):
                place = h * n + (j ^ k)
                top = stats_refs[k][place : place + 1, :] + slope_of(slopes_ref, h, bases[k].shape[1]) * bases[k]
                best = top if best is None else jnp.maximum(best, top)
            row.append(best)
        tops.append(row)
    return tops, bases[0]


def sums_kernel(n, slopes_ref, val_ref, score_ref, gt_ref, *refs):
    top_refs, (stats_ref, out_ref, expo_ref) = refs[:n], refs[n:]
    heads, tokens, lats = score_ref.shape
    rows = lats // n
    tops, base = merged_tops(n, heads, slopes_ref, top_refs)
    for h in range(heads):
        slope = slope_of(slopes_ref, h, rows)
        top = jnp.concatenate([t - slope * base for t in tops[h]], axis=1)
        norm = out = None
        for c in range(tokens // STEP):
            part = slice(c * STEP, (c + 1) * STEP)
            expo = jnp.exp2((score_ref[h, part, :] - top) * UNIT)
            expo_ref[h, part, :] = expo
            term = tn(val_ref[part, head_cols(h)], expo.astype(BF16))
            part_norm = jnp.sum(expo, axis=0, keepdims=True)
            out = term if out is None else out + term
            norm = part_norm if norm is None else norm + part_norm
        out_ref[head_cols(h), :] = out
        delta = jnp.sum(gt_ref[head_cols(h), :].astype(F32) * out, axis=0, keepdims=True)
        for j in range(n):
            cols = slice(j * rows, (j + 1) * rows)
            stats_ref[h * n + j : h * n + j + 1, :] = norm[:, cols]
            place = heads * n + h * n + j
            stats_ref[place : place + 1, :] = delta[:, cols]


def write_messages(i, rows, sums_ref, send_refs):
    for j, ref in enumerate(send_refs, 1):
        steps, exponent = encode(sums_ref[:, j * rows : (j + 1) * rows])
        ref[head_cols(i), :] = to_code(steps)
        place = slice(ref.shape[0] - 16, ref.shape[0])
        exponents = jnp.broadcast_to(exponent, (16, rows))
        if i:
            row = lax.broadcasted_iota(jnp.int32, (16, rows), 0)
            exponents = jnp.where(row < i, from_code(ref[place, :]), exponents)
        ref[place, :] = to_code(exponents)


def read_message(ref, i):
    exponents = from_code(ref[ref.shape[0] - 16 :, :])
    return decode(from_code(ref[head_cols(i), :]), exponents[i : i + 1, :])


def merged_sums(n, heads, stats_refs):
    norms, deltas = [], []
    for h in range(heads):
        norm_row, delta_row = [], []
        for j in range(n):
            norm = delta = None
            for k in range(n):
                place = h * n + (j ^ k)
                a = stats_refs[k][place : place + 1, :]
                b = stats_refs[k][heads * n + place : heads * n + place + 1, :]
                norm = a if norm is None else norm + a
                delta = b if delta is None else delta + b
            norm_row.append(norm)
            delta_row.append(delta)
        norms.append(jnp.concatenate(norm_row, axis=1))
        deltas.append(jnp.concatenate(delta_row, axis=1))
    return norms, deltas


def rows_kernel(n, bounds_ref, slopes_ref, key_ref, expo_ref, dprod_ref, out_ref, *refs):
    top_refs, sum_refs, refs = refs[:n], refs[n : 2 * n], refs[2 * n :]
    own_ref, grad_ref, slope_ref = refs[:3]
    send_refs = refs[3 : n + 2]
    (episode_ref,) = refs[n + 2 :]
    heads, tokens, lats = expo_ref.shape
    rows = lats // n
    _, base = merged_tops(n, heads, slopes_ref, top_refs)
    norms, deltas = merged_sums(n, heads, sum_refs)
    fill_episode(bounds_ref, episode_ref, base[:, :128])
    for h in range(heads):
        inverse = 1.0 / norms[h]
        mean = deltas[h] * inverse
        slope = jnp.zeros((1, 128), F32)
        dq = None
        for c in range(tokens // STEP):
            part = slice(c * STEP, (c + 1) * STEP)
            score_grad = expo_ref[h, part, :] * inverse * (dprod_ref[h, part, :] - mean)
            folded = score_grad[:, :128]
            for i in range(1, lats // 128):
                folded = folded + score_grad[:, i * 128 : (i + 1) * 128]
            slope = slope + jnp.sum(folded * episode_ref[part, :], axis=0, keepdims=True)
            score_grad_b = score_grad.astype(BF16)
            grad_ref[h, part, :] = score_grad_b
            term = tn(key_ref[part, head_cols(h)], score_grad_b)
            dq = term if dq is None else dq + term
        own_ref[head_cols(h), :] = dq[:, :rows]
        write_messages(2 * h, rows, dq, send_refs)
        write_messages(2 * h + 1, rows, out_ref[head_cols(h), :], send_refs)
        total = jnp.sum(slope, axis=1, keepdims=True)
        slope_ref[:, h * 2 * HEAD : (h + 1) * 2 * HEAD] = jnp.broadcast_to(total, (8, 2 * HEAD))


def tokens_kernel(n, expo_ref, grad_ref, qt_ref, gt_ref, *refs):
    sum_refs, tok_ref = refs[:n], refs[-1]
    heads, tokens, lats = expo_ref.shape
    norms, _ = merged_sums(n, heads, sum_refs)
    for h in range(heads):
        inverse = 1.0 / norms[h]
        at = h * 2 * HEAD
        for c in range(tokens // STEP):
            part = slice(c * STEP, (c + 1) * STEP)
            probs = (expo_ref[h, part, :] * inverse).astype(BF16)
            keys = SCALE * nt(qt_ref[head_cols(h), :], grad_ref[h, part, :])
            tok_ref[at : at + HEAD, part] = keys.astype(BF16)
            tok_ref[at + HEAD : at + 2 * HEAD, part] = nt(gt_ref[head_cols(h), :], probs).astype(BF16)


def weights_kernel(n, inp_ref, tok_ref, slope_ref, _, keep_ref, *refs):
    give_refs, weight_ref = refs[:n], refs[n]
    _, half, _ = weight_ref.shape
    piece = half // n
    for i in range(2):
        side = inp_ref[:, i * half : (i + 1) * half]
        weight_ref[i] = lax.dot_general(side, tok_ref[...], (((0,), (1,)), ((), ())), preferred_element_type=F32)
    core, me = lax.axis_index("dp"), lax.axis_index("seq")
    for k, give_ref in enumerate(give_refs):
        rows = pl.ds(pl.multiple_of((me ^ k) * piece, piece), piece)
        keep_ref[k, :piece, :] = weight_ref[core, rows, :]
        give_ref[:piece, :] = weight_ref[1 - core, rows, :]
    keep_ref[0, piece:, :] = slope_ref[...]
    give_refs[0][piece:, :] = slope_ref[...]


def pair_kernel(n, heads, keep_ref, *refs):
    got_refs, own_ref, send_refs = refs[:n], refs[-n], refs[1 - n :]
    piece = keep_ref.shape[1] - 8
    width = 2 * HEAD
    own_ref[...] = keep_ref[0] + got_refs[0][...]
    digits = []
    for h in range(heads):
        value = own_ref[piece : piece + 1, h * width : (h + 1) * width]
        steps, exponent = encode(value)
        left = value * (jnp.exp2(-exponent) * CODE_MAX) - steps
        digits += [exponent, steps, jnp.round(left * CODE_MAX)]
    for k in range(1, n):
        total = keep_ref[k, :piece, :] + got_refs[k][...]
        exponents = []
        for h in range(heads):
            steps, exponent = encode(total[:, h * width : (h + 1) * width])
            send_refs[k - 1][h * piece : (h + 1) * piece, :] = to_code(steps)
            exponents.append(exponent)
        send_refs[k - 1][heads * piece :, :] = to_code(stack_rows(exponents + digits, 16, width))


def attended_kernel(n, heads, out_ref, *refs):
    got_refs, sum_refs, att_ref = refs[: n - 1], refs[n - 1 : 2 * n - 1], refs[2 * n - 1]
    rows = att_ref.shape[1]
    norms, _ = merged_sums(n, heads, sum_refs)
    for h in range(heads):
        total = out_ref[head_cols(h), :rows]
        for ref in got_refs:
            total = total + read_message(ref, 2 * h + 1)
        total = total / norms[h][:, :rows]
        att_ref[0, :, head_cols(h)] = total.T.astype(BF16)


def last_kernel(n, heads, own_ref, weight_ref, *refs):
    got_refs, part_refs = refs[: n - 1], refs[n - 1 : 2 * n - 2]
    grad_ref, key_ref, val_ref, slope_ref = refs[2 * n - 2 :]
    for h in range(heads):
        total = own_ref[head_cols(h), :]
        for ref in got_refs:
            total = total + read_message(ref, 2 * h)
        grad_ref[0, :, head_cols(h)] = (SCALE * total).T.astype(BF16)
    piece = weight_ref.shape[0] - 8
    width = 2 * HEAD
    extras = [from_code(ref[heads * piece :, :]) for ref in part_refs]
    for h in range(heads):
        cols = slice(h * width, (h + 1) * width)
        total = weight_ref[:piece, cols]
        slope = weight_ref[piece : piece + 1, cols]
        for ref, extra in zip(part_refs, extras):
            total = total + decode(from_code(ref[h * piece : (h + 1) * piece, :]), extra[h : h + 1, :])
            place = heads + 3 * h
            exponent, steps, left = (extra[place + i : place + i + 1, :] for i in range(3))
            slope = slope + decode(steps + left * (1.0 / CODE_MAX), exponent)
        key_ref[:, head_cols(h)] = total[:, :HEAD]
        val_ref[:, head_cols(h)] = total[:, HEAD:]
        slope_ref[h] = slope[0, 0]


def call(kernel, name, outs, args, us, scratch=(), smem=0, limit=12 << 20, ins=None, out_specs=None):
    return pl.pallas_call(
        kernel,
        out_shape=[jax.ShapeDtypeStruct(shape, dtype) for shape, dtype in outs],
        in_specs=ins or [SMEM] * smem + [VMEM] * (len(args) - smem),
        out_specs=out_specs or [VMEM] * len(outs),
        scratch_shapes=list(scratch),
        compiler_params=pltpu.CompilerParams(vmem_limit_bytes=limit),
        cost_estimate=pl.CostEstimate(flops=int(us * 1.1e9), bytes_accessed=1 << 16, transcendentals=0),
        name=name,
    )(*args)


def per_device_blocks(n, tokens, levels, boundaries, level_table, w_key, w_value, slopes, queries, cotangent):
    toks, channels = tokens.shape[1:]
    rows, width = queries.shape[1:]
    heads = width // HEAD
    lats = n * rows
    peers = range(1, n)
    q_all = [queries] + [swap(queries, "seq", k, n) for k in peers]
    prep_args = (tokens, levels, level_table, w_key, w_value)
    inputs, keys, values, grad = call(
        prep_kernel,
        "prep",
        [((toks, channels), BF16), ((toks, width), BF16), ((toks, width), BF16), (cotangent.shape, BF16)],
        [pltpu.with_memory_space_constraint(x, pltpu.HBM) for x in (*prep_args, cotangent)],
        3,
        [pltpu.VMEM(a.shape, a.dtype) for a in prep_args] + [pltpu.SemaphoreType.DMA((5 + toks // CHUNK,))],
        ins=[pl.BlockSpec(memory_space=pltpu.HBM)] * 6,
    )
    g_all = [grad] + [swap(grad, "seq", k, n) for k in peers]
    stat_rows = -(-(heads * n + 1) // 8) * 8
    square = ((heads, toks, lats), F32)
    top_own, scores = call(
        functools.partial(top_kernel, n),
        "tops",
        [((stat_rows, rows), F32), square],
        (boundaries, slopes, keys, *q_all),
        2,
        [pltpu.VMEM((toks, 128), BF16)],
        2,
        limit=LIM_T << 20,
    )
    tops = [top_own] + [swap(top_own, "seq", k, n) for k in peers]
    q_turned, g_turned = call(
        functools.partial(turn_kernel, n),
        "turn",
        [((width, lats), BF16), ((width, lats), BF16)],
        (*q_all, cotangent, *g_all[1:]),
        1,
    )
    sums = call(
        functools.partial(sums_kernel, n),
        "sums",
        [((2 * heads * n, rows), F32), ((width, lats), F32), square],
        (slopes, values, scores, g_turned, *tops),
        2,
        smem=1,
        limit=LIM_S << 20,
    )
    norms = [sums[0]] + [swap(sums[0], "seq", k, n) for k in peers]
    (dprod,) = call(dprod_kernel, "dprod", [square], (values, g_turned, sums[0]), 2, limit=LIM_D << 20)
    own_dq, score_grads, slope_terms, *sends = call(
        functools.partial(rows_kernel, n),
        "rows",
        [((width, rows), F32), ((heads, toks, lats), BF16), ((8, 2 * width), F32)]
        + [((2 * width + 16, rows), I16)] * (n - 1),
        (boundaries, slopes, keys, sums[2], dprod, sums[1], *tops, *norms),
        3,
        [pltpu.VMEM((toks, 128), F32)],
        2,
        limit=LIM_G << 20,
    )
    blocks = [swap(x, "seq", k, n) for k, x in zip(peers, sends)]
    half = channels // 2
    (tok_grads,) = call(
        functools.partial(tokens_kernel, n),
        "tokens",
        [((2 * width, toks), BF16)],
        (sums[2], score_grads, q_turned, g_turned, *norms),
        3,
        limit=LIM_G << 20,
    )
    piece = half // n
    weights = call(
        functools.partial(weights_kernel, n),
        "weights",
        [((n, piece + 8, 2 * width), F32), ((piece + 8, 2 * width), F32)] + [((piece, 2 * width), F32)] * (n - 1),
        (inputs, tok_grads, slope_terms, blocks[0]),
        1,
        [pltpu.VMEM((2, half, 2 * width), F32)],
        limit=LIM_G << 20,
    )
    got = [swap(x, "dp", 1, 2) for x in weights[1:]]
    (attended,) = call(
        functools.partial(attended_kernel, n, heads),
        "attended",
        [((1, rows, width), BF16)],
        (sums[1], *blocks, *norms),
        1,
    )
    pair = call(
        functools.partial(pair_kernel, n, heads),
        "pair",
        [((piece + 8, 2 * width), F32)] + [((heads * piece + 16, 2 * HEAD), I16)] * (n - 1),
        (weights[0], *got, blocks[1]),
        0.3,
    )
    parts = [swap(pair[k], "seq", k, n) for k in peers]
    last = call(
        functools.partial(last_kernel, n, heads),
        "last",
        [((1, rows, width), BF16), ((piece, width), F32), ((piece, width), F32), ((heads,), F32)],
        (own_dq, pair[0], *blocks, *parts),
        1,
        out_specs=[VMEM] * 3 + [SMEM],
    )
    return (attended, *last)


def carried_in(part, axis, combine, identity):
    place = lax.axis_index(axis)
    gathered = lax.all_gather(part, axis)
    state = jnp.zeros_like(part) + jnp.asarray(identity, part.dtype)

    def one(step, state):
        return combine(state, lax.dynamic_index_in_dim(gathered, step, 0, False))

    return lax.fori_loop(0, place, one, state)


def add_counts(earlier, later):
    return earlier + later


def per_device_general(tokens, levels, boundaries, level_table, w_key, w_value, slopes, queries, cotangent):
    scale = HEAD ** (-0.5)
    raw = tokens[0].astype(jnp.float32)
    centered = raw - jnp.mean(raw, axis=1, keepdims=True)
    normed = centered / jnp.sqrt(jnp.mean(centered * centered, axis=1, keepdims=True) + 1e-05)
    lookup = jnp.take(level_table, levels[0], axis=0)
    inputs = (normed + lookup).astype(jnp.bfloat16)
    keys = jnp.dot(inputs, w_key, preferred_element_type=jnp.float32).astype(jnp.bfloat16)
    values = jnp.dot(inputs, w_value, preferred_element_type=jnp.float32).astype(jnp.bfloat16)
    bounds = boundaries[0]
    has = (bounds < BLOCK).astype(jnp.int32)
    earlier = carried_in(jnp.sum(has).reshape(1), "seq", add_counts, jnp.zeros((1,), jnp.int32))
    before = earlier[0] + jnp.cumsum(has) - has
    position = jnp.arange(BLOCK, dtype=jnp.int32)
    inside = (position[None, :] >= bounds[:, None]).astype(jnp.int32)
    episode = (before[:, None] + inside).reshape(-1).astype(jnp.float32)
    query_all, grad_all = (
        lax.all_gather(queries[0], "seq", axis=0, tiled=True),
        lax.all_gather(cotangent[0], "seq", axis=0, tiled=True),
    )
    latents = query_all.shape[0]
    heads = w_key.shape[1] // HEAD
    tok_rows = keys.shape[0]
    own_rows = queries.shape[1]
    start = lax.axis_index("seq") * own_rows
    query_heads = query_all.reshape(latents, heads, HEAD)
    grad_heads = grad_all.reshape(latents, heads, HEAD)
    key_heads = keys.reshape(tok_rows, heads, HEAD)
    value_heads = values.reshape(tok_rows, heads, HEAD)
    score = (
        jnp.einsum("nhd,thd->hnt", query_heads, key_heads, preferred_element_type=jnp.float32)
        * scale
    )
    score = score + slopes[:, None, None] * episode[None, None, :]
    top = lax.pmax(jnp.max(score, axis=2), "seq")
    expo = jnp.exp(score - top[:, :, None])
    part_norm = jnp.sum(expo, axis=2)
    part_out = jnp.einsum(
        "hnt,thd->nhd", expo.astype(jnp.bfloat16), value_heads, preferred_element_type=jnp.float32
    ).reshape(latents, heads * HEAD)
    grad_f32 = grad_all.astype(jnp.float32)
    summed, total = lax.psum((part_out, part_norm), "seq")
    mixed = (summed.reshape(latents, heads, HEAD) / total.T[:, :, None]).reshape(
        latents, heads * HEAD
    )
    delta = jnp.sum((grad_f32 * mixed).reshape(latents, heads, HEAD), axis=2).T
    own_mixed = lax.dynamic_slice_in_dim(mixed, start, own_rows, 0)
    attended = own_mixed.astype(jnp.bfloat16)[None]
    probs = expo / total[:, :, None]
    probs_b = probs.astype(jnp.bfloat16)
    value_tok = (
        jnp.einsum("hnt,nhd->thd", probs_b, grad_heads, preferred_element_type=jnp.float32)
        .astype(jnp.bfloat16)
        .reshape(tok_rows, heads * HEAD)
    )
    dprod = jnp.einsum("nhd,thd->hnt", grad_heads, value_heads, preferred_element_type=jnp.float32)
    score_grad = probs * (dprod - delta[:, :, None])
    slope_part = jnp.sum(score_grad * episode[None, None, :], axis=(1, 2))
    score_grad_b = score_grad.astype(jnp.bfloat16)
    query_part = (
        scale
        * jnp.einsum("hnt,thd->nhd", score_grad_b, key_heads, preferred_element_type=jnp.float32)
    ).reshape(latents, heads * HEAD)
    key_tok = (
        (
            scale
            * jnp.einsum(
                "hnt,nhd->thd", score_grad_b, query_heads, preferred_element_type=jnp.float32
            )
        )
        .astype(jnp.bfloat16)
        .reshape(tok_rows, heads * HEAD)
    )
    query_grad = lax.psum_scatter(query_part, "seq", scatter_dimension=0, tiled=True).astype(
        jnp.bfloat16
    )[None]
    key_part = jnp.dot(inputs.T, key_tok, preferred_element_type=jnp.float32)
    value_part = jnp.dot(inputs.T, value_tok, preferred_element_type=jnp.float32)
    key_weight_grad, value_weight_grad = (
        lax.psum_scatter(key_part, ("dp", "seq"), scatter_dimension=0, tiled=True),
        lax.psum_scatter(value_part, ("dp", "seq"), scatter_dimension=0, tiled=True),
    )
    slope_grad = lax.psum(slope_part, ("dp", "seq"))
    return (attended, query_grad, key_weight_grad, value_weight_grad, slope_grad)


def solution(mesh):
    n = mesh.shape["seq"]

    def per_device(*args):
        rows = args[7].shape[1]
        if n in (2, 4, 8) and mesh.shape["dp"] == 2 and rows % 128 == 0:
            return per_device_blocks(n, *args)
        return per_device_general(*args)

    return jax.shard_map(
        per_device,
        mesh=mesh,
        in_specs=(
            P("dp", "seq", None),
            P("dp", "seq"),
            P("dp", "seq"),
            P(),
            P(None, "tensor"),
            P(None, "tensor"),
            P("tensor"),
            P("dp", "seq", "tensor"),
            P("dp", "seq", "tensor"),
        ),
        out_specs=(
            P("dp", "seq", "tensor"),
            P("dp", "seq", "tensor"),
            P(("dp", "seq"), "tensor"),
            P(("dp", "seq"), "tensor"),
            P("tensor"),
        ),
        check_vma=False,
    )
```

```python
import functools

import jax
import jax.numpy as jnp
from jax import lax
from jax.experimental import pallas as pl
from jax.experimental.pallas import tpu as pltpu
from jax.sharding import PartitionSpec as P

HEAD = 128
BLOCK = 128
LOG2E = 1.4426950408889634
CODE_MAX = 32000.0
TINY = 1e-30
CHUNK = 512
STEP = 256
LIM_P, LIM_T, LIM_D, LIM_S, LIM_G = 55, 8, 8, 16, 16
SCALE = HEAD ** (-0.5)
UNIT = SCALE * LOG2E

F32 = jnp.float32
BF16 = jnp.bfloat16
I16 = jnp.int16
VMEM = pl.BlockSpec(memory_space=pltpu.VMEM)
SMEM = pl.BlockSpec(memory_space=pltpu.SMEM)


def nn(a, b):
    return lax.dot_general(a, b, (((1,), (0,)), ((), ())), preferred_element_type=F32)


def nt(a, b):
    return lax.dot_general(a, b, (((1,), (1,)), ((), ())), preferred_element_type=F32)


def tn(a, b):
    return lax.dot_general(a, b, (((0,), (0,)), ((), ())), preferred_element_type=F32)


def head_cols(h):
    return slice(h * HEAD, (h + 1) * HEAD)


def swap(x, axis, k, n):
    return lax.ppermute(x, axis, [(i, i ^ k) for i in range(n)])


def encode(x):
    most = jnp.maximum(jnp.max(jnp.abs(x), axis=0, keepdims=True), TINY)
    exponent = jnp.ceil(jnp.log2(most))
    steps = jnp.round(x * (jnp.exp2(-exponent) * CODE_MAX))
    return steps, exponent


def decode(steps, exponent):
    return steps * (jnp.exp2(exponent) * (1.0 / CODE_MAX))


def to_code(x):
    return x.astype(jnp.int32).astype(I16)


def from_code(x):
    return x.astype(jnp.int32).astype(F32)


def stack_rows(rows, total, width):
    place = lax.broadcasted_iota(jnp.int32, (total, width), 0)
    out = jnp.zeros((total, width), F32)
    for i, row in enumerate(rows):
        out = jnp.where(place == i, row, out)
    return out


def prep_kernel(tok_hbm, lev_hbm, table_hbm, wk_hbm, wv_hbm, g_hbm, inp_ref, key_ref, val_ref, g_ref, *scratch):
    tok_ref, lev_ref, table_ref, wk_ref, wv_ref, sems = scratch
    first = [(table_hbm, table_ref), (lev_hbm, lev_ref), (wk_hbm, wk_ref), (wv_hbm, wv_ref), (g_hbm, g_ref)]
    parts = [slice(c * CHUNK, (c + 1) * CHUNK) for c in range(tok_ref.shape[1] // CHUNK)]
    pairs = first + [(tok_hbm.at[:, part, :], tok_ref.at[:, part, :]) for part in parts]
    copies = [pltpu.make_async_copy(src, dst, sems.at[i]) for i, (src, dst) in enumerate(pairs)]
    for copy in copies:
        copy.start()
    for copy in copies[: len(first)]:
        copy.wait()
    table = table_ref[...]
    hi = table.astype(BF16)
    rest = table - hi.astype(F32)
    mid = rest.astype(BF16)
    low = (rest - mid.astype(F32)).astype(BF16)
    levels = table.shape[0]
    for c, rows in enumerate(parts):
        copies[len(first) + c].wait()
        raw = tok_ref[0, rows, :].astype(F32)
        centered = raw - jnp.mean(raw, axis=1, keepdims=True)
        normed = centered / jnp.sqrt(jnp.mean(centered * centered, axis=1, keepdims=True) + 1e-05)
        ids = lev_ref[0:1, rows]
        pick = (lax.broadcasted_iota(jnp.int32, (levels, CHUNK), 0) == ids).astype(F32).astype(BF16)
        lookup = (tn(pick, low) + tn(pick, mid)) + tn(pick, hi)
        inputs = (normed + lookup).astype(BF16)
        inp_ref[rows, :] = inputs
        key_ref[rows, :] = nn(inputs, wk_ref[...]).astype(BF16)
        val_ref[rows, :] = nn(inputs, wv_ref[...]).astype(BF16)


def three(x):
    hi = x.astype(BF16).astype(F32)
    mid = (x - hi).astype(BF16).astype(F32)
    return [hi, mid, x - hi - mid]


def fill_episode(bounds_ref, episode_ref, base):
    before = jnp.int32(0)
    shape = (BLOCK, episode_ref.shape[1])
    place = lax.broadcasted_iota(jnp.int32, shape, 0)
    for b in range(bounds_ref.shape[1]):
        bound = bounds_ref[0, b]
        episode = base + (before + (place >= bound).astype(jnp.int32)).astype(F32)
        episode_ref[b * BLOCK : (b + 1) * BLOCK, :] = episode.astype(episode_ref.dtype)
        before = before + (bound < BLOCK).astype(jnp.int32)
    return before


def slope_of(slopes_ref, h, width):
    return jnp.full((1, width), slopes_ref[h] * (1.0 / SCALE), F32)


def top_kernel(n, bounds_ref, slopes_ref, key_ref, *refs):
    q_refs, (stats_ref, score_ref, side_ref) = refs[:n], refs[n:]
    rows = q_refs[0].shape[1]
    tokens, width = key_ref.shape
    heads = width // HEAD
    starts = fill_episode(bounds_ref, side_ref, 0.0)
    lane = lax.broadcasted_iota(jnp.int32, (rows, 128), 1)
    for h in range(heads):
        beside = jnp.zeros((rows, 128), F32)
        for i, term in enumerate(three(slope_of(slopes_ref, h, 128))):
            beside = jnp.where(lane == i, term, beside)
        beside = beside.astype(BF16)
        keys = jnp.concatenate([key_ref[:, head_cols(h)], side_ref[...]], axis=1)
        for j in range(n):
            query = jnp.concatenate([q_refs[j][0, :, head_cols(h)], beside], axis=1)
            score = nt(keys, query)
            score_ref[h, :, j * rows : (j + 1) * rows] = score
            stats_ref[h * n + j : h * n + j + 1, :] = jnp.max(score, axis=0, keepdims=True)
    stats_ref[heads * n : heads * n + 1, :] = jnp.zeros((1, rows), F32) + starts.astype(F32)


def turn_kernel(n, *refs):
    q_refs, g_refs, (qt_ref, gt_ref) = refs[:n], refs[n : 2 * n], refs[2 * n :]
    rows = q_refs[0].shape[1]
    for j in range(n):
        cols = slice(j * rows, (j + 1) * rows)
        qt_ref[:, cols] = q_refs[j][0].astype(F32).T.astype(BF16)
        gt_ref[:, cols] = g_refs[j][0].astype(F32).T.astype(BF16)


def dprod_kernel(val_ref, gt_ref, dprod_ref):
    for h in range(dprod_ref.shape[0]):
        dprod_ref[h] = nn(val_ref[:, head_cols(h)], gt_ref[head_cols(h), :])


def merged_tops(n, heads, slopes_ref, stats_refs):
    me = lax.axis_index("seq")
    counts = [ref[heads * n : heads * n + 1, :] for ref in stats_refs]
    bases = []
    for k in range(n):
        base = jnp.zeros_like(counts[0])
        for j in range(n):
            earlier = ((me ^ j) < (me ^ k)).astype(F32)
            base = base + earlier * counts[j]
        bases.append(base)
    tops = []
    for h in range(heads):
        row = []
        for j in range(n):
            best = None
            for k in range(n):
                place = h * n + (j ^ k)
                top = stats_refs[k][place : place + 1, :] + slope_of(slopes_ref, h, bases[k].shape[1]) * bases[k]
                best = top if best is None else jnp.maximum(best, top)
            row.append(best)
        tops.append(row)
    return tops, bases[0]


def sums_kernel(n, slopes_ref, val_ref, score_ref, gt_ref, _, *refs):
    top_refs, (stats_ref, own_ref, expo_ref), send_refs = refs[:n], refs[n : n + 3], refs[n + 3 :]
    heads, tokens, lats = score_ref.shape
    rows = lats // n
    tops, base = merged_tops(n, heads, slopes_ref, top_refs)
    for h in range(heads):
        slope = slope_of(slopes_ref, h, rows)
        top = jnp.concatenate([t - slope * base for t in tops[h]], axis=1)
        norm = out = None
        for c in range(tokens // STEP):
            part = slice(c * STEP, (c + 1) * STEP)
            expo = jnp.exp2((score_ref[h, part, :] - top) * UNIT)
            expo_ref[h, part, :] = expo
            term = tn(val_ref[part, head_cols(h)], expo.astype(BF16))
            part_norm = jnp.sum(expo, axis=0, keepdims=True)
            out = term if out is None else out + term
            norm = part_norm if norm is None else norm + part_norm
        own_ref[head_cols(h), :] = out[:, :rows]
        write_messages(h, rows, out, send_refs)
        delta = jnp.sum(gt_ref[head_cols(h), :].astype(F32) * out, axis=0, keepdims=True)
        for j in range(n):
            cols = slice(j * rows, (j + 1) * rows)
            stats_ref[h * n + j : h * n + j + 1, :] = norm[:, cols]
            place = heads * n + h * n + j
            stats_ref[place : place + 1, :] = delta[:, cols]


def write_messages(i, rows, sums_ref, send_refs):
    for j, ref in enumerate(send_refs, 1):
        steps, exponent = encode(sums_ref[:, j * rows : (j + 1) * rows])
        ref[head_cols(i), :] = to_code(steps)
        place = slice(ref.shape[0] - 16, ref.shape[0])
        exponents = jnp.broadcast_to(exponent, (16, rows))
        if i:
            row = lax.broadcasted_iota(jnp.int32, (16, rows), 0)
            exponents = jnp.where(row < i, from_code(ref[place, :]), exponents)
        ref[place, :] = to_code(exponents)


def read_message(ref, i):
    exponents = from_code(ref[ref.shape[0] - 16 :, :])
    return decode(from_code(ref[head_cols(i), :]), exponents[i : i + 1, :])


def merged_sums(n, heads, stats_refs):
    norms, deltas = [], []
    for h in range(heads):
        norm_row, delta_row = [], []
        for j in range(n):
            norm = delta = None
            for k in range(n):
                place = h * n + (j ^ k)
                a = stats_refs[k][place : place + 1, :]
                b = stats_refs[k][heads * n + place : heads * n + place + 1, :]
                norm = a if norm is None else norm + a
                delta = b if delta is None else delta + b
            norm_row.append(norm)
            delta_row.append(delta)
        norms.append(jnp.concatenate(norm_row, axis=1))
        deltas.append(jnp.concatenate(delta_row, axis=1))
    return norms, deltas


def rows_kernel(n, bounds_ref, slopes_ref, key_ref, expo_ref, dprod_ref, *refs):
    top_refs, sum_refs, refs = refs[:n], refs[n : 2 * n], refs[2 * n :]
    own_ref, grad_ref, slope_ref = refs[:3]
    send_refs = refs[3 : n + 2]
    (episode_ref,) = refs[n + 2 :]
    heads, tokens, lats = expo_ref.shape
    rows = lats // n
    _, base = merged_tops(n, heads, slopes_ref, top_refs)
    norms, deltas = merged_sums(n, heads, sum_refs)
    fill_episode(bounds_ref, episode_ref, base[:, :128])
    for h in range(heads):
        inverse = 1.0 / norms[h]
        mean = deltas[h] * inverse
        slope = jnp.zeros((1, 128), F32)
        dq = None
        for c in range(tokens // STEP):
            part = slice(c * STEP, (c + 1) * STEP)
            score_grad = expo_ref[h, part, :] * inverse * (dprod_ref[h, part, :] - mean)
            folded = score_grad[:, :128]
            for i in range(1, lats // 128):
                folded = folded + score_grad[:, i * 128 : (i + 1) * 128]
            slope = slope + jnp.sum(folded * episode_ref[part, :], axis=0, keepdims=True)
            score_grad_b = score_grad.astype(BF16)
            grad_ref[h, part, :] = score_grad_b
            term = tn(key_ref[part, head_cols(h)], score_grad_b)
            dq = term if dq is None else dq + term
        own_ref[head_cols(h), :] = dq[:, :rows]
        write_messages(h, rows, dq, send_refs)
        total = jnp.sum(slope, axis=1, keepdims=True)
        slope_ref[:, h * 2 * HEAD : (h + 1) * 2 * HEAD] = jnp.broadcast_to(total, (8, 2 * HEAD))


def tokens_kernel(n, expo_ref, grad_ref, qt_ref, gt_ref, *refs):
    sum_refs, tok_ref = refs[:n], refs[-1]
    heads, tokens, lats = expo_ref.shape
    norms, _ = merged_sums(n, heads, sum_refs)
    for h in range(heads):
        inverse = 1.0 / norms[h]
        at = h * 2 * HEAD
        for c in range(tokens // STEP):
            part = slice(c * STEP, (c + 1) * STEP)
            probs = (expo_ref[h, part, :] * inverse).astype(BF16)
            keys = SCALE * nt(qt_ref[head_cols(h), :], grad_ref[h, part, :])
            tok_ref[at : at + HEAD, part] = keys.astype(BF16)
            tok_ref[at + HEAD : at + 2 * HEAD, part] = nt(gt_ref[head_cols(h), :], probs).astype(BF16)


def weights_kernel(n, inp_ref, tok_ref, slope_ref, _, keep_ref, *refs):
    give_refs, weight_ref = refs[:n], refs[n]
    _, half, _ = weight_ref.shape
    piece = half // n
    for i in range(2):
        side = inp_ref[:, i * half : (i + 1) * half]
        weight_ref[i] = lax.dot_general(side, tok_ref[...], (((0,), (1,)), ((), ())), preferred_element_type=F32)
    core, me = lax.axis_index("dp"), lax.axis_index("seq")
    for k, give_ref in enumerate(give_refs):
        rows = pl.ds(pl.multiple_of((me ^ k) * piece, piece), piece)
        keep_ref[k, :piece, :] = weight_ref[core, rows, :]
        give_ref[:piece, :] = weight_ref[1 - core, rows, :]
    keep_ref[0, piece:, :] = slope_ref[...]
    give_refs[0][piece:, :] = slope_ref[...]


def pair_kernel(n, heads, keep_ref, *refs):
    got_refs, own_ref, send_refs = refs[:n], refs[-n], refs[1 - n :]
    piece = keep_ref.shape[1] - 8
    width = 2 * HEAD
    own_ref[...] = keep_ref[0] + got_refs[0][...]
    digits = []
    for h in range(heads):
        value = own_ref[piece : piece + 1, h * width : (h + 1) * width]
        steps, exponent = encode(value)
        left = value * (jnp.exp2(-exponent) * CODE_MAX) - steps
        digits += [exponent, steps, jnp.round(left * CODE_MAX)]
    for k in range(1, n):
        total = keep_ref[k, :piece, :] + got_refs[k][...]
        exponents = []
        for h in range(heads):
            steps, exponent = encode(total[:, h * width : (h + 1) * width])
            send_refs[k - 1][h * piece : (h + 1) * piece, :] = to_code(steps)
            exponents.append(exponent)
        send_refs[k - 1][heads * piece :, :] = to_code(stack_rows(exponents + digits, 16, width))


def latents_kernel(n, heads, out_ref, own_ref, *refs):
    others = n - 1
    att_refs, dq_refs, sum_refs = refs[:others], refs[others : 2 * others], refs[2 * others : -2]
    att_ref, grad_ref = refs[-2:]
    rows = att_ref.shape[1]
    norms, _ = merged_sums(n, heads, sum_refs)
    for h in range(heads):
        total = out_ref[head_cols(h), :]
        for ref in att_refs:
            total = total + read_message(ref, h)
        grad = own_ref[head_cols(h), :]
        for ref in dq_refs:
            grad = grad + read_message(ref, h)
        total = total / norms[h][:, :rows]
        att_ref[0, :, head_cols(h)] = total.T.astype(BF16)
        grad_ref[0, :, head_cols(h)] = (SCALE * grad).T.astype(BF16)


def last_kernel(n, heads, weight_ref, *refs):
    part_refs, (key_ref, val_ref, slope_ref) = refs[: n - 1], refs[n - 1 :]
    piece = weight_ref.shape[0] - 8
    width = 2 * HEAD
    extras = [from_code(ref[heads * piece :, :]) for ref in part_refs]
    for h in range(heads):
        cols = slice(h * width, (h + 1) * width)
        total = weight_ref[:piece, cols]
        slope = weight_ref[piece : piece + 1, cols]
        for ref, extra in zip(part_refs, extras):
            total = total + decode(from_code(ref[h * piece : (h + 1) * piece, :]), extra[h : h + 1, :])
            place = heads + 3 * h
            exponent, steps, left = (extra[place + i : place + i + 1, :] for i in range(3))
            slope = slope + decode(steps + left * (1.0 / CODE_MAX), exponent)
        key_ref[:, head_cols(h)] = total[:, :HEAD]
        val_ref[:, head_cols(h)] = total[:, HEAD:]
        slope_ref[h] = slope[0, 0]


def call(kernel, name, outs, args, us, scratch=(), smem=0, limit=12 << 20, ins=None, out_specs=None):
    return pl.pallas_call(
        kernel,
        out_shape=[jax.ShapeDtypeStruct(shape, dtype) for shape, dtype in outs],
        in_specs=ins or [SMEM] * smem + [VMEM] * (len(args) - smem),
        out_specs=out_specs or [VMEM] * len(outs),
        scratch_shapes=list(scratch),
        compiler_params=pltpu.CompilerParams(vmem_limit_bytes=limit),
        cost_estimate=pl.CostEstimate(flops=int(us * 1.1e9), bytes_accessed=1 << 16, transcendentals=0),
        name=name,
    )(*args)


def per_device_blocks(n, tokens, levels, boundaries, level_table, w_key, w_value, slopes, queries, cotangent):
    toks, channels = tokens.shape[1:]
    rows, width = queries.shape[1:]
    heads = width // HEAD
    lats = n * rows
    peers = range(1, n)
    q_all = [queries] + [swap(queries, "seq", k, n) for k in peers]
    prep_args = (tokens, levels, level_table, w_key, w_value)
    inputs, keys, values, grad = call(
        prep_kernel,
        "prep",
        [((toks, channels), BF16), ((toks, width), BF16), ((toks, width), BF16), (cotangent.shape, BF16)],
        [pltpu.with_memory_space_constraint(x, pltpu.HBM) for x in (*prep_args, cotangent)],
        3,
        [pltpu.VMEM(a.shape, a.dtype) for a in prep_args] + [pltpu.SemaphoreType.DMA((5 + toks // CHUNK,))],
        ins=[pl.BlockSpec(memory_space=pltpu.HBM)] * 6,
    )
    g_all = [grad] + [swap(grad, "seq", k, n) for k in peers]
    stat_rows = -(-(heads * n + 1) // 8) * 8
    square = ((heads, toks, lats), F32)
    block = ((width + 16, rows), I16)
    top_own, scores = call(
        functools.partial(top_kernel, n),
        "tops",
        [((stat_rows, rows), F32), square],
        (boundaries, slopes, keys, *q_all),
        2,
        [pltpu.VMEM((toks, 128), BF16)],
        2,
        limit=LIM_T << 20,
    )
    tops = [top_own] + [swap(top_own, "seq", k, n) for k in peers]
    q_turned, g_turned = call(
        functools.partial(turn_kernel, n),
        "turn",
        [((width, lats), BF16), ((width, lats), BF16)],
        (*q_all, cotangent, *g_all[1:]),
        1,
    )
    (dprod,) = call(dprod_kernel, "dprod", [square], (values, g_turned), 2, limit=LIM_D << 20)
    sums = call(
        functools.partial(sums_kernel, n),
        "sums",
        [((2 * heads * n, rows), F32), ((width, rows), F32), square] + [block] * (n - 1),
        (slopes, values, scores, g_turned, dprod, *tops),
        2,
        smem=1,
        limit=LIM_S << 20,
    )
    norms = [sums[0]] + [swap(sums[0], "seq", k, n) for k in peers]
    outs = [swap(sums[2 + k], "seq", k, n) for k in peers]
    own_dq, score_grads, slope_terms, *sends = call(
        functools.partial(rows_kernel, n),
        "rows",
        [((width, rows), F32), ((heads, toks, lats), BF16), ((8, 2 * width), F32)]
        + [block] * (n - 1),
        (boundaries, slopes, keys, sums[2], dprod, *tops, *norms),
        3,
        [pltpu.VMEM((toks, 128), F32)],
        2,
        limit=LIM_G << 20,
    )
    dqs = [swap(x, "seq", k, n) for k, x in zip(peers, sends)]
    half = channels // 2
    (tok_grads,) = call(
        functools.partial(tokens_kernel, n),
        "tokens",
        [((2 * width, toks), BF16)],
        (sums[2], score_grads, q_turned, g_turned, *norms, *outs),
        3,
        limit=LIM_G << 20,
    )
    piece = half // n
    weights = call(
        functools.partial(weights_kernel, n),
        "weights",
        [((n, piece + 8, 2 * width), F32), ((piece + 8, 2 * width), F32)] + [((piece, 2 * width), F32)] * (n - 1),
        (inputs, tok_grads, slope_terms, dqs[0]),
        1,
        [pltpu.VMEM((2, half, 2 * width), F32)],
        limit=LIM_G << 20,
    )
    got = [swap(x, "dp", 1, 2) for x in weights[1:]]
    latents = call(
        functools.partial(latents_kernel, n, heads),
        "latents",
        [((1, rows, width), BF16)] * 2,
        (sums[1], own_dq, *outs, *dqs, *norms),
        1,
    )
    pair = call(
        functools.partial(pair_kernel, n, heads),
        "pair",
        [((piece + 8, 2 * width), F32)] + [((heads * piece + 16, 2 * HEAD), I16)] * (n - 1),
        (weights[0], *got, dqs[1]),
        0.3,
    )
    parts = [swap(pair[k], "seq", k, n) for k in peers]
    last = call(
        functools.partial(last_kernel, n, heads),
        "last",
        [((piece, width), F32), ((piece, width), F32), ((heads,), F32)],
        (pair[0], *parts),
        1,
        out_specs=[VMEM] * 2 + [SMEM],
    )
    return (*latents, *last)


def carried_in(part, axis, combine, identity):
    place = lax.axis_index(axis)
    gathered = lax.all_gather(part, axis)
    state = jnp.zeros_like(part) + jnp.asarray(identity, part.dtype)

    def one(step, state):
        return combine(state, lax.dynamic_index_in_dim(gathered, step, 0, False))

    return lax.fori_loop(0, place, one, state)


def add_counts(earlier, later):
    return earlier + later


def per_device_general(tokens, levels, boundaries, level_table, w_key, w_value, slopes, queries, cotangent):
    scale = HEAD ** (-0.5)
    raw = tokens[0].astype(jnp.float32)
    centered = raw - jnp.mean(raw, axis=1, keepdims=True)
    normed = centered / jnp.sqrt(jnp.mean(centered * centered, axis=1, keepdims=True) + 1e-05)
    lookup = jnp.take(level_table, levels[0], axis=0)
    inputs = (normed + lookup).astype(jnp.bfloat16)
    keys = jnp.dot(inputs, w_key, preferred_element_type=jnp.float32).astype(jnp.bfloat16)
    values = jnp.dot(inputs, w_value, preferred_element_type=jnp.float32).astype(jnp.bfloat16)
    bounds = boundaries[0]
    has = (bounds < BLOCK).astype(jnp.int32)
    earlier = carried_in(jnp.sum(has).reshape(1), "seq", add_counts, jnp.zeros((1,), jnp.int32))
    before = earlier[0] + jnp.cumsum(has) - has
    position = jnp.arange(BLOCK, dtype=jnp.int32)
    inside = (position[None, :] >= bounds[:, None]).astype(jnp.int32)
    episode = (before[:, None] + inside).reshape(-1).astype(jnp.float32)
    query_all, grad_all = (
        lax.all_gather(queries[0], "seq", axis=0, tiled=True),
        lax.all_gather(cotangent[0], "seq", axis=0, tiled=True),
    )
    latents = query_all.shape[0]
    heads = w_key.shape[1] // HEAD
    tok_rows = keys.shape[0]
    own_rows = queries.shape[1]
    start = lax.axis_index("seq") * own_rows
    query_heads = query_all.reshape(latents, heads, HEAD)
    grad_heads = grad_all.reshape(latents, heads, HEAD)
    key_heads = keys.reshape(tok_rows, heads, HEAD)
    value_heads = values.reshape(tok_rows, heads, HEAD)
    score = (
        jnp.einsum("nhd,thd->hnt", query_heads, key_heads, preferred_element_type=jnp.float32)
        * scale
    )
    score = score + slopes[:, None, None] * episode[None, None, :]
    top = lax.pmax(jnp.max(score, axis=2), "seq")
    expo = jnp.exp(score - top[:, :, None])
    part_norm = jnp.sum(expo, axis=2)
    part_out = jnp.einsum(
        "hnt,thd->nhd", expo.astype(jnp.bfloat16), value_heads, preferred_element_type=jnp.float32
    ).reshape(latents, heads * HEAD)
    grad_f32 = grad_all.astype(jnp.float32)
    summed, total = lax.psum((part_out, part_norm), "seq")
    mixed = (summed.reshape(latents, heads, HEAD) / total.T[:, :, None]).reshape(
        latents, heads * HEAD
    )
    delta = jnp.sum((grad_f32 * mixed).reshape(latents, heads, HEAD), axis=2).T
    own_mixed = lax.dynamic_slice_in_dim(mixed, start, own_rows, 0)
    attended = own_mixed.astype(jnp.bfloat16)[None]
    probs = expo / total[:, :, None]
    probs_b = probs.astype(jnp.bfloat16)
    value_tok = (
        jnp.einsum("hnt,nhd->thd", probs_b, grad_heads, preferred_element_type=jnp.float32)
        .astype(jnp.bfloat16)
        .reshape(tok_rows, heads * HEAD)
    )
    dprod = jnp.einsum("nhd,thd->hnt", grad_heads, value_heads, preferred_element_type=jnp.float32)
    score_grad = probs * (dprod - delta[:, :, None])
    slope_part = jnp.sum(score_grad * episode[None, None, :], axis=(1, 2))
    score_grad_b = score_grad.astype(jnp.bfloat16)
    query_part = (
        scale
        * jnp.einsum("hnt,thd->nhd", score_grad_b, key_heads, preferred_element_type=jnp.float32)
    ).reshape(latents, heads * HEAD)
    key_tok = (
        (
            scale
            * jnp.einsum(
                "hnt,nhd->thd", score_grad_b, query_heads, preferred_element_type=jnp.float32
            )
        )
        .astype(jnp.bfloat16)
        .reshape(tok_rows, heads * HEAD)
    )
    query_grad = lax.psum_scatter(query_part, "seq", scatter_dimension=0, tiled=True).astype(
        jnp.bfloat16
    )[None]
    key_part = jnp.dot(inputs.T, key_tok, preferred_element_type=jnp.float32)
    value_part = jnp.dot(inputs.T, value_tok, preferred_element_type=jnp.float32)
    key_weight_grad, value_weight_grad = (
        lax.psum_scatter(key_part, ("dp", "seq"), scatter_dimension=0, tiled=True),
        lax.psum_scatter(value_part, ("dp", "seq"), scatter_dimension=0, tiled=True),
    )
    slope_grad = lax.psum(slope_part, ("dp", "seq"))
    return (attended, query_grad, key_weight_grad, value_weight_grad, slope_grad)


def solution(mesh):
    n = mesh.shape["seq"]

    def per_device(*args):
        rows = args[7].shape[1]
        if n in (2, 4, 8) and mesh.shape["dp"] == 2 and rows % 128 == 0:
            return per_device_blocks(n, *args)
        return per_device_general(*args)

    return jax.shard_map(
        per_device,
        mesh=mesh,
        in_specs=(
            P("dp", "seq", None),
            P("dp", "seq"),
            P("dp", "seq"),
            P(),
            P(None, "tensor"),
            P(None, "tensor"),
            P("tensor"),
            P("dp", "seq", "tensor"),
            P("dp", "seq", "tensor"),
        ),
        out_specs=(
            P("dp", "seq", "tensor"),
            P("dp", "seq", "tensor"),
            P(("dp", "seq"), "tensor"),
            P(("dp", "seq"), "tensor"),
            P("tensor"),
        ),
        check_vma=False,
    )
```

```python
import functools

import jax
import jax.numpy as jnp
from jax import lax
from jax.experimental import pallas as pl
from jax.experimental.pallas import tpu as pltpu
from jax.sharding import PartitionSpec as P

HEAD = 128
BLOCK = 128
LOG2E = 1.4426950408889634
CODE_MAX = 32000.0
TINY = 1e-30
WHOLE = 1.5 * 2.0**23
CHUNK = 512
STEP = 256
GIVES = 2
LIM_P, LIM_T, LIM_D, LIM_S, LIM_G = 55, 8, 8, 16, 16
SCALE = HEAD ** (-0.5)
UNIT = SCALE * LOG2E

F32 = jnp.float32
BF16 = jnp.bfloat16
I16 = jnp.int16
VMEM = pl.BlockSpec(memory_space=pltpu.VMEM)
SMEM = pl.BlockSpec(memory_space=pltpu.SMEM)


def nn(a, b):
    return lax.dot_general(a, b, (((1,), (0,)), ((), ())), preferred_element_type=F32)


def nt(a, b):
    return lax.dot_general(a, b, (((1,), (1,)), ((), ())), preferred_element_type=F32)


def tn(a, b):
    return lax.dot_general(a, b, (((0,), (0,)), ((), ())), preferred_element_type=F32)


def head_cols(h):
    return slice(h * HEAD, (h + 1) * HEAD)


def swap(x, axis, k, n):
    return lax.ppermute(x, axis, [(i, i ^ k) for i in range(n)])


def encode(x):
    most = jnp.maximum(jnp.max(jnp.abs(x), axis=0, keepdims=True), TINY)
    exponent = jnp.ceil(jnp.log2(most))
    return whole(x * (jnp.exp2(-exponent) * CODE_MAX)), exponent


def whole(x):
    return (x + WHOLE) - WHOLE


def decode(steps, exponent):
    return steps * (jnp.exp2(exponent) * (1.0 / CODE_MAX))


def to_code(x):
    return x.astype(jnp.int32).astype(I16)


def from_code(x):
    return x.astype(jnp.int32).astype(F32)


def stack_rows(rows, total, width):
    place = lax.broadcasted_iota(jnp.int32, (total, width), 0)
    out = jnp.zeros((total, width), F32)
    for i, row in enumerate(rows):
        out = jnp.where(place == i, row, out)
    return out


def prep_kernel(tok_hbm, lev_hbm, table_hbm, wk_hbm, wv_hbm, g_hbm, inp_ref, key_ref, val_ref, g_ref, *scratch):
    tok_ref, lev_ref, table_ref, wk_ref, wv_ref, sems = scratch
    first = [(table_hbm, table_ref), (lev_hbm, lev_ref), (wk_hbm, wk_ref), (wv_hbm, wv_ref), (g_hbm, g_ref)]
    parts = [slice(c * CHUNK, (c + 1) * CHUNK) for c in range(tok_ref.shape[1] // CHUNK)]
    pairs = first + [(tok_hbm.at[:, part, :], tok_ref.at[:, part, :]) for part in parts]
    copies = [pltpu.make_async_copy(src, dst, sems.at[i]) for i, (src, dst) in enumerate(pairs)]
    for copy in copies:
        copy.start()
    for copy in copies[: len(first)]:
        copy.wait()
    table = table_ref[...]
    hi = table.astype(BF16)
    rest = table - hi.astype(F32)
    mid = rest.astype(BF16)
    low = (rest - mid.astype(F32)).astype(BF16)
    levels = table.shape[0]
    for c, rows in enumerate(parts):
        copies[len(first) + c].wait()
        raw = tok_ref[0, rows, :].astype(F32)
        centered = raw - jnp.mean(raw, axis=1, keepdims=True)
        normed = centered / jnp.sqrt(jnp.mean(centered * centered, axis=1, keepdims=True) + 1e-05)
        ids = lev_ref[0:1, rows]
        pick = (lax.broadcasted_iota(jnp.int32, (levels, CHUNK), 0) == ids).astype(F32).astype(BF16)
        lookup = (tn(pick, low) + tn(pick, mid)) + tn(pick, hi)
        inputs = (normed + lookup).astype(BF16)
        inp_ref[rows, :] = inputs
        key_ref[rows, :] = nn(inputs, wk_ref[...]).astype(BF16)
        val_ref[rows, :] = nn(inputs, wv_ref[...]).astype(BF16)


def three(x):
    hi = x.astype(BF16).astype(F32)
    mid = (x - hi).astype(BF16).astype(F32)
    return [hi, mid, x - hi - mid]


def fill_episode(bounds_ref, episode_ref, base):
    before = jnp.int32(0)
    shape = (BLOCK, episode_ref.shape[1])
    place = lax.broadcasted_iota(jnp.int32, shape, 0)
    for b in range(bounds_ref.shape[1]):
        bound = bounds_ref[0, b]
        episode = base + (before + (place >= bound).astype(jnp.int32)).astype(F32)
        episode_ref[b * BLOCK : (b + 1) * BLOCK, :] = episode.astype(episode_ref.dtype)
        before = before + (bound < BLOCK).astype(jnp.int32)
    return before


def slope_of(slopes_ref, h, width):
    return jnp.full((1, width), slopes_ref[h] * (1.0 / SCALE), F32)


def top_kernel(n, bounds_ref, slopes_ref, key_ref, *refs):
    q_refs, (stats_ref, score_ref, side_ref) = refs[:n], refs[n:]
    rows = q_refs[0].shape[1]
    tokens, width = key_ref.shape
    heads = width // HEAD
    starts = fill_episode(bounds_ref, side_ref, 0.0)
    lane = lax.broadcasted_iota(jnp.int32, (rows, 128), 1)
    for h in range(heads):
        beside = jnp.zeros((rows, 128), F32)
        for i, term in enumerate(three(slope_of(slopes_ref, h, 128))):
            beside = jnp.where(lane == i, term, beside)
        beside = beside.astype(BF16)
        keys = jnp.concatenate([key_ref[:, head_cols(h)], side_ref[...]], axis=1)
        for j in range(n):
            query = jnp.concatenate([q_refs[j][0, :, head_cols(h)], beside], axis=1)
            score = nt(keys, query)
            score_ref[h, :, j * rows : (j + 1) * rows] = score
            stats_ref[h * n + j : h * n + j + 1, :] = jnp.max(score, axis=0, keepdims=True)
    stats_ref[heads * n : heads * n + 1, :] = jnp.zeros((1, rows), F32) + starts.astype(F32)


def turn_kernel(n, *refs):
    q_refs, g_refs, (qt_ref, gt_ref) = refs[:n], refs[n : 2 * n], refs[2 * n :]
    rows = q_refs[0].shape[1]
    for j in range(n):
        cols = slice(j * rows, (j + 1) * rows)
        qt_ref[:, cols] = q_refs[j][0].astype(F32).T.astype(BF16)
        gt_ref[:, cols] = g_refs[j][0].astype(F32).T.astype(BF16)


def dprod_kernel(val_ref, gt_ref, dprod_ref):
    for h in range(dprod_ref.shape[0]):
        dprod_ref[h] = nn(val_ref[:, head_cols(h)], gt_ref[head_cols(h), :])


def merged_tops(n, heads, slopes_ref, stats_refs):
    me = lax.axis_index("seq")
    counts = [ref[heads * n : heads * n + 1, :] for ref in stats_refs]
    bases = []
    for k in range(n):
        base = jnp.zeros_like(counts[0])
        for j in range(n):
            earlier = ((me ^ j) < (me ^ k)).astype(F32)
            base = base + earlier * counts[j]
        bases.append(base)
    tops = []
    for h in range(heads):
        row = []
        for j in range(n):
            best = None
            for k in range(n):
                place = h * n + (j ^ k)
                top = stats_refs[k][place : place + 1, :] + slope_of(slopes_ref, h, bases[k].shape[1]) * bases[k]
                best = top if best is None else jnp.maximum(best, top)
            row.append(best)
        tops.append(row)
    return tops, bases[0]


def sums_kernel(n, slopes_ref, val_ref, score_ref, gt_ref, _, *refs):
    top_refs, (stats_ref, out_ref, expo_ref) = refs[:n], refs[n:]
    heads, tokens, lats = score_ref.shape
    rows = lats // n
    tops, base = merged_tops(n, heads, slopes_ref, top_refs)
    for h in range(heads):
        slope = slope_of(slopes_ref, h, rows)
        top = jnp.concatenate([t - slope * base for t in tops[h]], axis=1)
        norm = out = None
        for c in range(tokens // STEP):
            part = slice(c * STEP, (c + 1) * STEP)
            expo = jnp.exp2((score_ref[h, part, :] - top) * UNIT)
            expo_ref[h, part, :] = expo
            term = tn(val_ref[part, head_cols(h)], expo.astype(BF16))
            part_norm = jnp.sum(expo, axis=0, keepdims=True)
            out = term if out is None else out + term
            norm = part_norm if norm is None else norm + part_norm
        out_ref[head_cols(h), :] = out
        delta = jnp.sum(gt_ref[head_cols(h), :].astype(F32) * out, axis=0, keepdims=True)
        for j in range(n):
            cols = slice(j * rows, (j + 1) * rows)
            stats_ref[h * n + j : h * n + j + 1, :] = norm[:, cols]
            place = heads * n + h * n + j
            stats_ref[place : place + 1, :] = delta[:, cols]


def write_messages(i, rows, sums_ref, send_refs):
    for j, ref in enumerate(send_refs, 1):
        steps, exponent = encode(sums_ref[:, j * rows : (j + 1) * rows])
        ref[head_cols(i), :] = to_code(steps)
        place = slice(ref.shape[0] - 16, ref.shape[0])
        exponents = jnp.broadcast_to(exponent, (16, rows))
        if i:
            row = lax.broadcasted_iota(jnp.int32, (16, rows), 0)
            exponents = jnp.where(row < i, from_code(ref[place, :]), exponents)
        ref[place, :] = to_code(exponents)


def read_message(ref, i):
    exponents = from_code(ref[ref.shape[0] - 16 :, :])
    return decode(from_code(ref[head_cols(i), :]), exponents[i : i + 1, :])


def merged_sums(n, heads, stats_refs):
    norms, deltas = [], []
    for h in range(heads):
        norm_row, delta_row = [], []
        for j in range(n):
            norm = delta = None
            for k in range(n):
                place = h * n + (j ^ k)
                a = stats_refs[k][place : place + 1, :]
                b = stats_refs[k][heads * n + place : heads * n + place + 1, :]
                norm = a if norm is None else norm + a
                delta = b if delta is None else delta + b
            norm_row.append(norm)
            delta_row.append(delta)
        norms.append(jnp.concatenate(norm_row, axis=1))
        deltas.append(jnp.concatenate(delta_row, axis=1))
    return norms, deltas


def rows_kernel(n, bounds_ref, slopes_ref, key_ref, expo_ref, dprod_ref, out_ref, *refs):
    top_refs, sum_refs, refs = refs[:n], refs[n : 2 * n], refs[2 * n :]
    own_ref, grad_ref, slope_ref = refs[:3]
    send_refs = refs[3 : n + 2]
    (episode_ref,) = refs[n + 2 :]
    heads, tokens, lats = expo_ref.shape
    rows = lats // n
    _, base = merged_tops(n, heads, slopes_ref, top_refs)
    norms, deltas = merged_sums(n, heads, sum_refs)
    fill_episode(bounds_ref, episode_ref, base[:, :128])
    for h in range(heads):
        inverse = 1.0 / norms[h]
        mean = deltas[h] * inverse
        slope = jnp.zeros((1, 128), F32)
        dq = None
        for c in range(tokens // STEP):
            part = slice(c * STEP, (c + 1) * STEP)
            score_grad = expo_ref[h, part, :] * inverse * (dprod_ref[h, part, :] - mean)
            folded = score_grad[:, :128]
            for i in range(1, lats // 128):
                folded = folded + score_grad[:, i * 128 : (i + 1) * 128]
            slope = slope + jnp.sum(folded * episode_ref[part, :], axis=0, keepdims=True)
            score_grad_b = score_grad.astype(BF16)
            grad_ref[h, part, :] = score_grad_b
            term = tn(key_ref[part, head_cols(h)], score_grad_b)
            dq = term if dq is None else dq + term
        own_ref[head_cols(h), :] = dq[:, :rows]
        write_messages(2 * h, rows, dq, send_refs)
        write_messages(2 * h + 1, rows, out_ref[head_cols(h), :], send_refs)
        total = jnp.sum(slope, axis=1, keepdims=True)
        slope_ref[:, h * 2 * HEAD : (h + 1) * 2 * HEAD] = jnp.broadcast_to(total, (8, 2 * HEAD))


def tokens_kernel(n, expo_ref, grad_ref, qt_ref, gt_ref, *refs):
    sum_refs, tok_ref = refs[:n], refs[-1]
    heads, tokens, lats = expo_ref.shape
    norms, _ = merged_sums(n, heads, sum_refs)
    for h in range(heads):
        inverse = 1.0 / norms[h]
        at = h * 2 * HEAD
        for c in range(tokens // STEP):
            part = slice(c * STEP, (c + 1) * STEP)
            probs = (expo_ref[h, part, :] * inverse).astype(BF16)
            keys = SCALE * nt(qt_ref[head_cols(h), :], grad_ref[h, part, :])
            tok_ref[at : at + HEAD, part] = keys.astype(BF16)
            tok_ref[at + HEAD : at + 2 * HEAD, part] = nt(gt_ref[head_cols(h), :], probs).astype(BF16)


def digits_of(value):
    steps, exponent = encode(value)
    left = value * (jnp.exp2(-exponent) * CODE_MAX) - steps
    return [exponent, steps, whole(left * CODE_MAX)]


def value_of(rows):
    return decode(rows[1] + rows[2] * (1.0 / CODE_MAX), rows[0])


def give_place(k):
    return min(k, GIVES - 1), max(k - GIVES + 1, 0)


def weights_kernel(n, inp_ref, tok_ref, slope_ref, *refs):
    keep_ref, *give_refs, weight_ref = refs[-2 - GIVES :]
    _, half, width = weight_ref.shape
    piece = half // n
    for i in range(2):
        side = inp_ref[:, i * half : (i + 1) * half]
        weight_ref[i] = lax.dot_general(side, tok_ref[...], (((0,), (1,)), ((), ())), preferred_element_type=F32)
    core, me = lax.axis_index("dp"), lax.axis_index("seq")
    steps, exponent = encode(weight_ref[1 - core])
    weight_ref[1 - core] = steps
    for k in range(n):
        rows = pl.ds(pl.multiple_of((me ^ k) * piece, piece), piece)
        keep_ref[k * piece : (k + 1) * piece, :] = weight_ref[core, rows, :]
        ref, at = give_refs[give_place(k)[0]], give_place(k)[1]
        ref[at * piece : (at + 1) * piece, :] = to_code(weight_ref[1 - core, rows, :])
    give_refs[0][piece : piece + 16, :] = to_code(stack_rows([exponent] + digits_of(slope_ref[0:1, :]), 16, width))


def pair_kernel(n, heads, keep_ref, slope_ref, *refs):
    got_refs, own_ref, send_refs = refs[:GIVES], refs[-n], refs[1 - n :]
    half = keep_ref.shape[0]
    piece = half // n
    width = 2 * HEAD
    extra = from_code(got_refs[0][piece : piece + 16, :])
    slope = slope_ref[0:1, :] + value_of([extra[i : i + 1, :] for i in range(1, 4)])
    own_ref[piece:, :] = jnp.broadcast_to(slope, (8, heads * width))
    digits = digits_of(slope)
    for k in range(n):
        ref, at = got_refs[give_place(k)[0]], give_place(k)[1]
        got = decode(from_code(ref[at * piece : (at + 1) * piece, :]), extra[0:1, :])
        total = keep_ref[k * piece : (k + 1) * piece, :] + got
        if k == 0:
            own_ref[:piece, :] = total
            continue
        steps, exponent = encode(total)
        rows = []
        for h in range(heads):
            cols = slice(h * width, (h + 1) * width)
            send_refs[k - 1][h * piece : (h + 1) * piece, :] = to_code(steps[:, cols])
            rows += [x[:, cols] for x in (exponent, *digits)]
        send_refs[k - 1][heads * piece :, :] = to_code(stack_rows(rows, 16, width))


def latents_kernel(n, heads, out_ref, own_ref, *refs):
    got_refs, sum_refs, (att_ref, grad_ref) = refs[: n - 1], refs[n - 1 : 2 * n - 1], refs[2 * n - 1 :]
    rows = att_ref.shape[1]
    norms, _ = merged_sums(n, heads, sum_refs)
    for h in range(heads):
        total = out_ref[head_cols(h), :rows]
        grad = own_ref[head_cols(h), :]
        for ref in got_refs:
            grad = grad + read_message(ref, 2 * h)
            total = total + read_message(ref, 2 * h + 1)
        total = total / norms[h][:, :rows]
        att_ref[0, :, head_cols(h)] = total.T.astype(BF16)
        grad_ref[0, :, head_cols(h)] = (SCALE * grad).T.astype(BF16)


def last_kernel(n, heads, weight_ref, *refs):
    part_refs, (key_ref, val_ref, slope_ref) = refs[: n - 1], refs[n - 1 :]
    piece = weight_ref.shape[0] - 8
    width = 2 * HEAD
    extras = [from_code(ref[heads * piece :, :]) for ref in part_refs]
    for h in range(heads):
        cols = slice(h * width, (h + 1) * width)
        total = weight_ref[:piece, cols]
        slope = weight_ref[piece : piece + 1, cols]
        for ref, extra in zip(part_refs, extras):
            exponent, *digits = (extra[4 * h + i : 4 * h + i + 1, :] for i in range(4))
            total = total + decode(from_code(ref[h * piece : (h + 1) * piece, :]), exponent)
            slope = slope + value_of(digits)
        key_ref[:, head_cols(h)] = total[:, :HEAD]
        val_ref[:, head_cols(h)] = total[:, HEAD:]
        slope_ref[h] = slope[0, 0]


def call(kernel, name, outs, args, us, scratch=(), smem=0, limit=12 << 20, ins=None, out_specs=None):
    return pl.pallas_call(
        kernel,
        out_shape=[jax.ShapeDtypeStruct(shape, dtype) for shape, dtype in outs],
        in_specs=ins or [SMEM] * smem + [VMEM] * (len(args) - smem),
        out_specs=out_specs or [VMEM] * len(outs),
        scratch_shapes=list(scratch),
        compiler_params=pltpu.CompilerParams(vmem_limit_bytes=limit),
        cost_estimate=pl.CostEstimate(flops=int(us * 1.1e9), bytes_accessed=1 << 16, transcendentals=0),
        name=name,
    )(*args)


def per_device_blocks(n, tokens, levels, boundaries, level_table, w_key, w_value, slopes, queries, cotangent):
    toks, channels = tokens.shape[1:]
    rows, width = queries.shape[1:]
    heads = width // HEAD
    lats = n * rows
    peers = range(1, n)
    q_all = [queries] + [swap(queries, "seq", k, n) for k in peers]
    prep_args = (tokens, levels, level_table, w_key, w_value)
    inputs, keys, values, grad = call(
        prep_kernel,
        "prep",
        [((toks, channels), BF16), ((toks, width), BF16), ((toks, width), BF16), (cotangent.shape, BF16)],
        [pltpu.with_memory_space_constraint(x, pltpu.HBM) for x in (*prep_args, cotangent)],
        3,
        [pltpu.VMEM(a.shape, a.dtype) for a in prep_args] + [pltpu.SemaphoreType.DMA((5 + toks // CHUNK,))],
        ins=[pl.BlockSpec(memory_space=pltpu.HBM)] * 6,
    )
    g_all = [grad] + [swap(grad, "seq", k, n) for k in peers]
    stat_rows = -(-(heads * n + 1) // 8) * 8
    square = ((heads, toks, lats), F32)
    block = ((2 * width + 16, rows), I16)
    top_own, scores = call(
        functools.partial(top_kernel, n),
        "tops",
        [((stat_rows, rows), F32), square],
        (boundaries, slopes, keys, *q_all),
        2,
        [pltpu.VMEM((toks, 128), BF16)],
        2,
        limit=LIM_T << 20,
    )
    tops = [top_own] + [swap(top_own, "seq", k, n) for k in peers]
    q_turned, g_turned = call(
        functools.partial(turn_kernel, n),
        "turn",
        [((width, lats), BF16), ((width, lats), BF16)],
        (*q_all, cotangent, *g_all[1:]),
        1,
    )
    (dprod,) = call(dprod_kernel, "dprod", [square], (values, g_turned), 2, limit=LIM_D << 20)
    sums = call(
        functools.partial(sums_kernel, n),
        "sums",
        [((2 * heads * n, rows), F32), ((width, lats), F32), square],
        (slopes, values, scores, g_turned, dprod, *tops),
        2,
        smem=1,
        limit=LIM_S << 20,
    )
    norms = [sums[0]] + [swap(sums[0], "seq", k, n) for k in peers]
    own_dq, score_grads, slope_terms, *sends = call(
        functools.partial(rows_kernel, n),
        "rows",
        [((width, rows), F32), ((heads, toks, lats), BF16), ((8, 2 * width), F32)]
        + [block] * (n - 1),
        (boundaries, slopes, keys, sums[2], dprod, sums[1], *tops, *norms),
        3,
        [pltpu.VMEM((toks, 128), F32)],
        2,
        limit=LIM_G << 20,
    )
    blocks = [swap(x, "seq", k, n) for k, x in zip(peers, sends)]
    half = channels // 2
    (tok_grads,) = call(
        functools.partial(tokens_kernel, n),
        "tokens",
        [((2 * width, toks), BF16)],
        (sums[2], score_grads, q_turned, g_turned, *norms),
        3,
        limit=LIM_G << 20,
    )
    piece = half // n
    weights = call(
        functools.partial(weights_kernel, n),
        "weights",
        [((half, 2 * width), F32), ((piece + 16, 2 * width), I16)]
        + [((piece, 2 * width), I16)] * (GIVES - 2)
        + [(((n - GIVES + 1) * piece, 2 * width), I16)],
        (inputs, tok_grads, slope_terms),
        1,
        [pltpu.VMEM((2, half, 2 * width), F32)],
        limit=LIM_G << 20,
    )
    got = [swap(x, "dp", 1, 2) for x in weights[1:]]
    latents = call(
        functools.partial(latents_kernel, n, heads),
        "latents",
        [((1, rows, width), BF16)] * 2,
        (sums[1], own_dq, *blocks, *norms),
        1,
    )
    pair = call(
        functools.partial(pair_kernel, n, heads),
        "pair",
        [((piece + 8, 2 * width), F32)] + [((heads * piece + 16, 2 * HEAD), I16)] * (n - 1),
        (weights[0], slope_terms, *got, blocks[0]),
        0.3,
    )
    parts = [swap(pair[k], "seq", k, n) for k in peers]
    last = call(
        functools.partial(last_kernel, n, heads),
        "last",
        [((piece, width), F32), ((piece, width), F32), ((heads,), F32)],
        (pair[0], *parts),
        1,
        out_specs=[VMEM] * 2 + [SMEM],
    )
    return (*latents, *last)


def carried_in(part, axis, combine, identity):
    place = lax.axis_index(axis)
    gathered = lax.all_gather(part, axis)
    state = jnp.zeros_like(part) + jnp.asarray(identity, part.dtype)

    def one(step, state):
        return combine(state, lax.dynamic_index_in_dim(gathered, step, 0, False))

    return lax.fori_loop(0, place, one, state)


def add_counts(earlier, later):
    return earlier + later


def per_device_general(tokens, levels, boundaries, level_table, w_key, w_value, slopes, queries, cotangent):
    scale = HEAD ** (-0.5)
    raw = tokens[0].astype(jnp.float32)
    centered = raw - jnp.mean(raw, axis=1, keepdims=True)
    normed = centered / jnp.sqrt(jnp.mean(centered * centered, axis=1, keepdims=True) + 1e-05)
    lookup = jnp.take(level_table, levels[0], axis=0)
    inputs = (normed + lookup).astype(jnp.bfloat16)
    keys = jnp.dot(inputs, w_key, preferred_element_type=jnp.float32).astype(jnp.bfloat16)
    values = jnp.dot(inputs, w_value, preferred_element_type=jnp.float32).astype(jnp.bfloat16)
    bounds = boundaries[0]
    has = (bounds < BLOCK).astype(jnp.int32)
    earlier = carried_in(jnp.sum(has).reshape(1), "seq", add_counts, jnp.zeros((1,), jnp.int32))
    before = earlier[0] + jnp.cumsum(has) - has
    position = jnp.arange(BLOCK, dtype=jnp.int32)
    inside = (position[None, :] >= bounds[:, None]).astype(jnp.int32)
    episode = (before[:, None] + inside).reshape(-1).astype(jnp.float32)
    query_all, grad_all = (
        lax.all_gather(queries[0], "seq", axis=0, tiled=True),
        lax.all_gather(cotangent[0], "seq", axis=0, tiled=True),
    )
    latents = query_all.shape[0]
    heads = w_key.shape[1] // HEAD
    tok_rows = keys.shape[0]
    own_rows = queries.shape[1]
    start = lax.axis_index("seq") * own_rows
    query_heads = query_all.reshape(latents, heads, HEAD)
    grad_heads = grad_all.reshape(latents, heads, HEAD)
    key_heads = keys.reshape(tok_rows, heads, HEAD)
    value_heads = values.reshape(tok_rows, heads, HEAD)
    score = (
        jnp.einsum("nhd,thd->hnt", query_heads, key_heads, preferred_element_type=jnp.float32)
        * scale
    )
    score = score + slopes[:, None, None] * episode[None, None, :]
    top = lax.pmax(jnp.max(score, axis=2), "seq")
    expo = jnp.exp(score - top[:, :, None])
    part_norm = jnp.sum(expo, axis=2)
    part_out = jnp.einsum(
        "hnt,thd->nhd", expo.astype(jnp.bfloat16), value_heads, preferred_element_type=jnp.float32
    ).reshape(latents, heads * HEAD)
    grad_f32 = grad_all.astype(jnp.float32)
    summed, total = lax.psum((part_out, part_norm), "seq")
    mixed = (summed.reshape(latents, heads, HEAD) / total.T[:, :, None]).reshape(
        latents, heads * HEAD
    )
    delta = jnp.sum((grad_f32 * mixed).reshape(latents, heads, HEAD), axis=2).T
    own_mixed = lax.dynamic_slice_in_dim(mixed, start, own_rows, 0)
    attended = own_mixed.astype(jnp.bfloat16)[None]
    probs = expo / total[:, :, None]
    probs_b = probs.astype(jnp.bfloat16)
    value_tok = (
        jnp.einsum("hnt,nhd->thd", probs_b, grad_heads, preferred_element_type=jnp.float32)
        .astype(jnp.bfloat16)
        .reshape(tok_rows, heads * HEAD)
    )
    dprod = jnp.einsum("nhd,thd->hnt", grad_heads, value_heads, preferred_element_type=jnp.float32)
    score_grad = probs * (dprod - delta[:, :, None])
    slope_part = jnp.sum(score_grad * episode[None, None, :], axis=(1, 2))
    score_grad_b = score_grad.astype(jnp.bfloat16)
    query_part = (
        scale
        * jnp.einsum("hnt,thd->nhd", score_grad_b, key_heads, preferred_element_type=jnp.float32)
    ).reshape(latents, heads * HEAD)
    key_tok = (
        (
            scale
            * jnp.einsum(
                "hnt,nhd->thd", score_grad_b, query_heads, preferred_element_type=jnp.float32
            )
        )
        .astype(jnp.bfloat16)
        .reshape(tok_rows, heads * HEAD)
    )
    query_grad = lax.psum_scatter(query_part, "seq", scatter_dimension=0, tiled=True).astype(
        jnp.bfloat16
    )[None]
    key_part = jnp.dot(inputs.T, key_tok, preferred_element_type=jnp.float32)
    value_part = jnp.dot(inputs.T, value_tok, preferred_element_type=jnp.float32)
    key_weight_grad, value_weight_grad = (
        lax.psum_scatter(key_part, ("dp", "seq"), scatter_dimension=0, tiled=True),
        lax.psum_scatter(value_part, ("dp", "seq"), scatter_dimension=0, tiled=True),
    )
    slope_grad = lax.psum(slope_part, ("dp", "seq"))
    return (attended, query_grad, key_weight_grad, value_weight_grad, slope_grad)


def solution(mesh):
    n = mesh.shape["seq"]

    def per_device(*args):
        toks, (rows, width) = args[0].shape[1], args[7].shape[1:]
        fits = rows % 128 == 0 and toks % CHUNK == 0 and toks // BLOCK <= 256 and width // HEAD <= 4
        if n in (2, 4, 8) and mesh.shape["dp"] == 2 and fits:
            return per_device_blocks(n, *args)
        return per_device_general(*args)

    return jax.shard_map(
        per_device,
        mesh=mesh,
        in_specs=(
            P("dp", "seq", None),
            P("dp", "seq"),
            P("dp", "seq"),
            P(),
            P(None, "tensor"),
            P(None, "tensor"),
            P("tensor"),
            P("dp", "seq", "tensor"),
            P("dp", "seq", "tensor"),
        ),
        out_specs=(
            P("dp", "seq", "tensor"),
            P("dp", "seq", "tensor"),
            P(("dp", "seq"), "tensor"),
            P(("dp", "seq"), "tensor"),
            P("tensor"),
        ),
        check_vma=False,
    )
```

```python
import functools

import jax
import jax.numpy as jnp
from jax import lax
from jax.experimental import pallas as pl
from jax.experimental.pallas import tpu as pltpu
from jax.sharding import PartitionSpec as P

HEAD = 128
BLOCK = 128
LOG2E = 1.4426950408889634
CODE_MAX = 32000.0
TINY = 1e-30
WHOLE = 1.5 * 2.0**23
CHUNK = 512
STEP = 256
GIVES = 2
LIM_P, LIM_T, LIM_D, LIM_S, LIM_G = 55, 8, 8, 16, 16
SCALE = HEAD ** (-0.5)
UNIT = SCALE * LOG2E

F32 = jnp.float32
BF16 = jnp.bfloat16
I16 = jnp.int16
VMEM = pl.BlockSpec(memory_space=pltpu.VMEM)
SMEM = pl.BlockSpec(memory_space=pltpu.SMEM)


def nn(a, b):
    return lax.dot_general(a, b, (((1,), (0,)), ((), ())), preferred_element_type=F32)


def nt(a, b):
    return lax.dot_general(a, b, (((1,), (1,)), ((), ())), preferred_element_type=F32)


def tn(a, b):
    return lax.dot_general(a, b, (((0,), (0,)), ((), ())), preferred_element_type=F32)


def head_cols(h):
    return slice(h * HEAD, (h + 1) * HEAD)


def swap(x, axis, k, n):
    return lax.ppermute(x, axis, [(i, i ^ k) for i in range(n)])


def encode(x):
    most = jnp.maximum(jnp.max(jnp.abs(x), axis=0, keepdims=True), TINY)
    exponent = jnp.ceil(jnp.log2(most))
    return whole(x * (jnp.exp2(-exponent) * CODE_MAX)), exponent


def whole(x):
    return (x + WHOLE) - WHOLE


def decode(steps, exponent):
    return steps * (jnp.exp2(exponent) * (1.0 / CODE_MAX))


def to_code(x):
    return x.astype(jnp.int32).astype(I16)


def from_code(x):
    return x.astype(jnp.int32).astype(F32)


def stack_rows(rows, total, width):
    place = lax.broadcasted_iota(jnp.int32, (total, width), 0)
    out = jnp.zeros((total, width), F32)
    for i, row in enumerate(rows):
        out = jnp.where(place == i, row, out)
    return out


def prep_kernel(tok_hbm, lev_hbm, table_hbm, wk_hbm, wv_hbm, g_hbm, inp_ref, key_ref, val_ref, g_ref, *scratch):
    tok_ref, lev_ref, table_ref, wk_ref, wv_ref, sems = scratch
    first = [(table_hbm, table_ref), (lev_hbm, lev_ref), (wk_hbm, wk_ref), (wv_hbm, wv_ref), (g_hbm, g_ref)]
    parts = [slice(c * CHUNK, (c + 1) * CHUNK) for c in range(tok_ref.shape[1] // CHUNK)]
    pairs = first + [(tok_hbm.at[:, part, :], tok_ref.at[:, part, :]) for part in parts]
    copies = [pltpu.make_async_copy(src, dst, sems.at[i]) for i, (src, dst) in enumerate(pairs)]
    for copy in copies:
        copy.start()
    for copy in copies[: len(first)]:
        copy.wait()
    table = table_ref[...]
    hi = table.astype(BF16)
    rest = table - hi.astype(F32)
    mid = rest.astype(BF16)
    low = (rest - mid.astype(F32)).astype(BF16)
    levels = table.shape[0]
    for c, rows in enumerate(parts):
        copies[len(first) + c].wait()
        raw = tok_ref[0, rows, :].astype(F32)
        centered = raw - jnp.mean(raw, axis=1, keepdims=True)
        normed = centered / jnp.sqrt(jnp.mean(centered * centered, axis=1, keepdims=True) + 1e-05)
        ids = lev_ref[0:1, rows]
        pick = (lax.broadcasted_iota(jnp.int32, (levels, CHUNK), 0) == ids).astype(F32).astype(BF16)
        lookup = (tn(pick, low) + tn(pick, mid)) + tn(pick, hi)
        inputs = (normed + lookup).astype(BF16)
        inp_ref[rows, :] = inputs
        key_ref[rows, :] = nn(inputs, wk_ref[...]).astype(BF16)
        val_ref[rows, :] = nn(inputs, wv_ref[...]).astype(BF16)


def three(x):
    hi = x.astype(BF16).astype(F32)
    mid = (x - hi).astype(BF16).astype(F32)
    return [hi, mid, x - hi - mid]


def fill_episode(bounds_ref, episode_ref, base):
    before = jnp.int32(0)
    shape = (BLOCK, episode_ref.shape[1])
    place = lax.broadcasted_iota(jnp.int32, shape, 0)
    for b in range(bounds_ref.shape[1]):
        bound = bounds_ref[0, b]
        episode = base + (before + (place >= bound).astype(jnp.int32)).astype(F32)
        episode_ref[b * BLOCK : (b + 1) * BLOCK, :] = episode.astype(episode_ref.dtype)
        before = before + (bound < BLOCK).astype(jnp.int32)
    return before


def slope_of(slopes_ref, h, width):
    return jnp.full((1, width), slopes_ref[h] * (1.0 / SCALE), F32)


def top_kernel(n, bounds_ref, slopes_ref, key_ref, *refs):
    q_refs, (stats_ref, score_ref, side_ref) = refs[:n], refs[n:]
    rows = q_refs[0].shape[1]
    tokens, width = key_ref.shape
    heads = width // HEAD
    starts = fill_episode(bounds_ref, side_ref, 0.0)
    lane = lax.broadcasted_iota(jnp.int32, (rows, 128), 1)
    for h in range(heads):
        beside = jnp.zeros((rows, 128), F32)
        for i, term in enumerate(three(slope_of(slopes_ref, h, 128))):
            beside = jnp.where(lane == i, term, beside)
        beside = beside.astype(BF16)
        keys = jnp.concatenate([key_ref[:, head_cols(h)], side_ref[...]], axis=1)
        for j in range(n):
            query = jnp.concatenate([q_refs[j][0, :, head_cols(h)], beside], axis=1)
            score = nt(keys, query)
            score_ref[h, :, j * rows : (j + 1) * rows] = score
            stats_ref[h * n + j : h * n + j + 1, :] = jnp.max(score, axis=0, keepdims=True)
    stats_ref[heads * n : heads * n + 1, :] = jnp.zeros((1, rows), F32) + starts.astype(F32)


def turn_kernel(n, *refs):
    q_refs, g_refs, (qt_ref, gt_ref) = refs[:n], refs[n : 2 * n], refs[2 * n :]
    rows = q_refs[0].shape[1]
    for j in range(n):
        cols = slice(j * rows, (j + 1) * rows)
        qt_ref[:, cols] = q_refs[j][0].astype(F32).T.astype(BF16)
        gt_ref[:, cols] = g_refs[j][0].astype(F32).T.astype(BF16)


def dprod_kernel(val_ref, gt_ref, dprod_ref):
    for h in range(dprod_ref.shape[0]):
        dprod_ref[h] = nn(val_ref[:, head_cols(h)], gt_ref[head_cols(h), :])


def merged_tops(n, heads, slopes_ref, stats_refs):
    me = lax.axis_index("seq")
    counts = [ref[heads * n : heads * n + 1, :] for ref in stats_refs]
    bases = []
    for k in range(n):
        base = jnp.zeros_like(counts[0])
        for j in range(n):
            earlier = ((me ^ j) < (me ^ k)).astype(F32)
            base = base + earlier * counts[j]
        bases.append(base)
    tops = []
    for h in range(heads):
        row = []
        for j in range(n):
            best = None
            for k in range(n):
                place = h * n + (j ^ k)
                top = stats_refs[k][place : place + 1, :] + slope_of(slopes_ref, h, bases[k].shape[1]) * bases[k]
                best = top if best is None else jnp.maximum(best, top)
            row.append(best)
        tops.append(row)
    return tops, bases[0]


def sums_kernel(n, slopes_ref, val_ref, score_ref, gt_ref, _, *refs):
    top_refs, (stats_ref, out_ref, expo_ref) = refs[:n], refs[n:]
    heads, tokens, lats = score_ref.shape
    rows = lats // n
    tops, base = merged_tops(n, heads, slopes_ref, top_refs)
    for h in range(heads):
        slope = slope_of(slopes_ref, h, rows)
        top = jnp.concatenate([t - slope * base for t in tops[h]], axis=1)
        norm = out = None
        for c in range(tokens // STEP):
            part = slice(c * STEP, (c + 1) * STEP)
            expo = jnp.exp2((score_ref[h, part, :] - top) * UNIT)
            expo_ref[h, part, :] = expo
            term = tn(val_ref[part, head_cols(h)], expo.astype(BF16))
            part_norm = jnp.sum(expo, axis=0, keepdims=True)
            out = term if out is None else out + term
            norm = part_norm if norm is None else norm + part_norm
        out_ref[head_cols(h), :] = out
        delta = jnp.sum(gt_ref[head_cols(h), :].astype(F32) * out, axis=0, keepdims=True)
        for j in range(n):
            cols = slice(j * rows, (j + 1) * rows)
            stats_ref[h * n + j : h * n + j + 1, :] = norm[:, cols]
            place = heads * n + h * n + j
            stats_ref[place : place + 1, :] = delta[:, cols]


def write_messages(i, rows, sums_ref, send_refs):
    for j, ref in enumerate(send_refs, 1):
        steps, exponent = encode(sums_ref[:, j * rows : (j + 1) * rows])
        ref[head_cols(i), :] = to_code(steps)
        place = slice(ref.shape[0] - 16, ref.shape[0])
        exponents = jnp.broadcast_to(exponent, (16, rows))
        if i:
            row = lax.broadcasted_iota(jnp.int32, (16, rows), 0)
            exponents = jnp.where(row < i, from_code(ref[place, :]), exponents)
        ref[place, :] = to_code(exponents)


def read_message(ref, i):
    exponents = from_code(ref[ref.shape[0] - 16 :, :])
    return decode(from_code(ref[head_cols(i), :]), exponents[i : i + 1, :])


def merged_sums(n, heads, stats_refs):
    norms, deltas = [], []
    for h in range(heads):
        norm_row, delta_row = [], []
        for j in range(n):
            norm = delta = None
            for k in range(n):
                place = h * n + (j ^ k)
                a = stats_refs[k][place : place + 1, :]
                b = stats_refs[k][heads * n + place : heads * n + place + 1, :]
                norm = a if norm is None else norm + a
                delta = b if delta is None else delta + b
            norm_row.append(norm)
            delta_row.append(delta)
        norms.append(jnp.concatenate(norm_row, axis=1))
        deltas.append(jnp.concatenate(delta_row, axis=1))
    return norms, deltas


def pack_kernel(n, out_ref, *send_refs):
    rows = out_ref.shape[1] // n
    for h in range(out_ref.shape[0] // HEAD):
        write_messages(h, rows, out_ref[head_cols(h), :], send_refs)


def rows_kernel(n, bounds_ref, slopes_ref, key_ref, expo_ref, dprod_ref, *refs):
    packed_refs, refs = refs[: n - 1], refs[n - 1 :]
    top_refs, sum_refs, refs = refs[:n], refs[n : 2 * n], refs[2 * n :]
    own_ref, grad_ref, slope_ref = refs[:3]
    send_refs = refs[3 : n + 2]
    (episode_ref,) = refs[n + 2 :]
    heads, tokens, lats = expo_ref.shape
    rows = lats // n
    _, base = merged_tops(n, heads, slopes_ref, top_refs)
    norms, deltas = merged_sums(n, heads, sum_refs)
    fill_episode(bounds_ref, episode_ref, base[:, :128])
    for h in range(heads):
        inverse = 1.0 / norms[h]
        mean = deltas[h] * inverse
        slope = jnp.zeros((1, 128), F32)
        dq = None
        for c in range(tokens // STEP):
            part = slice(c * STEP, (c + 1) * STEP)
            score_grad = expo_ref[h, part, :] * inverse * (dprod_ref[h, part, :] - mean)
            folded = score_grad[:, :128]
            for i in range(1, lats // 128):
                folded = folded + score_grad[:, i * 128 : (i + 1) * 128]
            slope = slope + jnp.sum(folded * episode_ref[part, :], axis=0, keepdims=True)
            score_grad_b = score_grad.astype(BF16)
            grad_ref[h, part, :] = score_grad_b
            term = tn(key_ref[part, head_cols(h)], score_grad_b)
            dq = term if dq is None else dq + term
        own_ref[head_cols(h), :] = dq[:, :rows]
        if h == 0:
            for ref, packed_ref in zip(send_refs, packed_refs):
                full = packed_ref.shape[0] - 16
                ref[:full, :] = packed_ref[:full, :]
                ref[2 * full :, :] = packed_ref[full:, :]
        write_messages(heads + h, rows, dq, send_refs)
        total = jnp.sum(slope, axis=1, keepdims=True)
        slope_ref[:, h * 2 * HEAD : (h + 1) * 2 * HEAD] = jnp.broadcast_to(total, (8, 2 * HEAD))


def tokens_kernel(n, expo_ref, grad_ref, qt_ref, gt_ref, *refs):
    sum_refs, tok_ref = refs[:n], refs[-1]
    heads, tokens, lats = expo_ref.shape
    norms, _ = merged_sums(n, heads, sum_refs)
    for h in range(heads):
        inverse = 1.0 / norms[h]
        at = h * 2 * HEAD
        for c in range(tokens // STEP):
            part = slice(c * STEP, (c + 1) * STEP)
            probs = (expo_ref[h, part, :] * inverse).astype(BF16)
            keys = SCALE * nt(qt_ref[head_cols(h), :], grad_ref[h, part, :])
            tok_ref[at : at + HEAD, part] = keys.astype(BF16)
            tok_ref[at + HEAD : at + 2 * HEAD, part] = nt(gt_ref[head_cols(h), :], probs).astype(BF16)


def digits_of(value):
    steps, exponent = encode(value)
    left = value * (jnp.exp2(-exponent) * CODE_MAX) - steps
    return [exponent, steps, whole(left * CODE_MAX)]


def value_of(rows):
    return decode(rows[1] + rows[2] * (1.0 / CODE_MAX), rows[0])


def give_place(k):
    return min(k, GIVES - 1), max(k - GIVES + 1, 0)


def weights_kernel(n, inp_ref, tok_ref, slope_ref, *refs):
    keep_ref, *give_refs, weight_ref = refs[-2 - GIVES :]
    _, half, width = weight_ref.shape
    piece = half // n
    for i in range(2):
        side = inp_ref[:, i * half : (i + 1) * half]
        weight_ref[i] = lax.dot_general(side, tok_ref[...], (((0,), (1,)), ((), ())), preferred_element_type=F32)
    core, me = lax.axis_index("dp"), lax.axis_index("seq")
    steps, exponent = encode(weight_ref[1 - core])
    weight_ref[1 - core] = steps
    for k in range(n):
        rows = pl.ds(pl.multiple_of((me ^ k) * piece, piece), piece)
        keep_ref[k * piece : (k + 1) * piece, :] = weight_ref[core, rows, :]
        ref, at = give_refs[give_place(k)[0]], give_place(k)[1]
        ref[at * piece : (at + 1) * piece, :] = to_code(weight_ref[1 - core, rows, :])
    give_refs[0][piece : piece + 16, :] = to_code(stack_rows([exponent] + digits_of(slope_ref[0:1, :]), 16, width))


def pair_kernel(n, heads, keep_ref, slope_ref, *refs):
    got_refs, own_ref, send_refs = refs[:GIVES], refs[-n], refs[1 - n :]
    half = keep_ref.shape[0]
    piece = half // n
    width = 2 * HEAD
    extra = from_code(got_refs[0][piece : piece + 16, :])
    slope = slope_ref[0:1, :] + value_of([extra[i : i + 1, :] for i in range(1, 4)])
    own_ref[piece:, :] = jnp.broadcast_to(slope, (8, heads * width))
    digits = digits_of(slope)
    for k in range(n):
        ref, at = got_refs[give_place(k)[0]], give_place(k)[1]
        got = decode(from_code(ref[at * piece : (at + 1) * piece, :]), extra[0:1, :])
        total = keep_ref[k * piece : (k + 1) * piece, :] + got
        if k == 0:
            own_ref[:piece, :] = total
            continue
        steps, exponent = encode(total)
        rows = []
        for h in range(heads):
            cols = slice(h * width, (h + 1) * width)
            send_refs[k - 1][h * piece : (h + 1) * piece, :] = to_code(steps[:, cols])
            rows += [x[:, cols] for x in (exponent, *digits)]
        send_refs[k - 1][heads * piece :, :] = to_code(stack_rows(rows, 16, width))


def latents_kernel(n, heads, out_ref, own_ref, *refs):
    got_refs, sum_refs, (att_ref, grad_ref) = refs[: n - 1], refs[n - 1 : 2 * n - 1], refs[2 * n - 1 :]
    rows = att_ref.shape[1]
    norms, _ = merged_sums(n, heads, sum_refs)
    for h in range(heads):
        total = out_ref[head_cols(h), :rows]
        grad = own_ref[head_cols(h), :]
        for ref in got_refs:
            grad = grad + read_message(ref, heads + h)
            total = total + read_message(ref, h)
        total = total / norms[h][:, :rows]
        att_ref[0, :, head_cols(h)] = total.T.astype(BF16)
        grad_ref[0, :, head_cols(h)] = (SCALE * grad).T.astype(BF16)


def last_kernel(n, heads, weight_ref, *refs):
    part_refs, (key_ref, val_ref, slope_ref) = refs[: n - 1], refs[n - 1 :]
    piece = weight_ref.shape[0] - 8
    width = 2 * HEAD
    extras = [from_code(ref[heads * piece :, :]) for ref in part_refs]
    for h in range(heads):
        cols = slice(h * width, (h + 1) * width)
        total = weight_ref[:piece, cols]
        slope = weight_ref[piece : piece + 1, cols]
        for ref, extra in zip(part_refs, extras):
            exponent, *digits = (extra[4 * h + i : 4 * h + i + 1, :] for i in range(4))
            total = total + decode(from_code(ref[h * piece : (h + 1) * piece, :]), exponent)
            slope = slope + value_of(digits)
        key_ref[:, head_cols(h)] = total[:, :HEAD]
        val_ref[:, head_cols(h)] = total[:, HEAD:]
        slope_ref[h] = slope[0, 0]


def call(kernel, name, outs, args, us, scratch=(), smem=0, limit=12 << 20, ins=None, out_specs=None):
    return pl.pallas_call(
        kernel,
        out_shape=[jax.ShapeDtypeStruct(shape, dtype) for shape, dtype in outs],
        in_specs=ins or [SMEM] * smem + [VMEM] * (len(args) - smem),
        out_specs=out_specs or [VMEM] * len(outs),
        scratch_shapes=list(scratch),
        compiler_params=pltpu.CompilerParams(vmem_limit_bytes=limit),
        cost_estimate=pl.CostEstimate(flops=int(us * 1.1e9), bytes_accessed=1 << 16, transcendentals=0),
        name=name,
    )(*args)


def per_device_blocks(n, tokens, levels, boundaries, level_table, w_key, w_value, slopes, queries, cotangent):
    toks, channels = tokens.shape[1:]
    rows, width = queries.shape[1:]
    heads = width // HEAD
    lats = n * rows
    peers = range(1, n)
    q_all = [queries] + [swap(queries, "seq", k, n) for k in peers]
    prep_args = (tokens, levels, level_table, w_key, w_value)
    inputs, keys, values, grad = call(
        prep_kernel,
        "prep",
        [((toks, channels), BF16), ((toks, width), BF16), ((toks, width), BF16), (cotangent.shape, BF16)],
        [pltpu.with_memory_space_constraint(x, pltpu.HBM) for x in (*prep_args, cotangent)],
        3,
        [pltpu.VMEM(a.shape, a.dtype) for a in prep_args] + [pltpu.SemaphoreType.DMA((5 + toks // CHUNK,))],
        ins=[pl.BlockSpec(memory_space=pltpu.HBM)] * 6,
    )
    g_all = [grad] + [swap(grad, "seq", k, n) for k in peers]
    stat_rows = -(-(heads * n + 1) // 8) * 8
    square = ((heads, toks, lats), F32)
    block = ((2 * width + 16, rows), I16)
    top_own, scores = call(
        functools.partial(top_kernel, n),
        "tops",
        [((stat_rows, rows), F32), square],
        (boundaries, slopes, keys, *q_all),
        2,
        [pltpu.VMEM((toks, 128), BF16)],
        2,
        limit=LIM_T << 20,
    )
    tops = [top_own] + [swap(top_own, "seq", k, n) for k in peers]
    q_turned, g_turned = call(
        functools.partial(turn_kernel, n),
        "turn",
        [((width, lats), BF16), ((width, lats), BF16)],
        (*q_all, cotangent, *g_all[1:]),
        1,
    )
    (dprod,) = call(dprod_kernel, "dprod", [square], (values, g_turned), 2, limit=LIM_D << 20)
    sums = call(
        functools.partial(sums_kernel, n),
        "sums",
        [((2 * heads * n, rows), F32), ((width, lats), F32), square],
        (slopes, values, scores, g_turned, dprod, *tops),
        2,
        smem=1,
        limit=LIM_S << 20,
    )
    norms = [sums[0]] + [swap(sums[0], "seq", k, n) for k in peers]
    packed = call(
        functools.partial(pack_kernel, n), "pack", [((width + 16, rows), I16)] * (n - 1), (sums[1],), 0.5
    )
    own_dq, score_grads, slope_terms, *sends = call(
        functools.partial(rows_kernel, n),
        "rows",
        [((width, rows), F32), ((heads, toks, lats), BF16), ((8, 2 * width), F32)]
        + [block] * (n - 1),
        (boundaries, slopes, keys, sums[2], dprod, *packed, *tops, *norms),
        3,
        [pltpu.VMEM((toks, 128), F32)],
        2,
        limit=LIM_G << 20,
    )
    blocks = [swap(x, "seq", k, n) for k, x in zip(peers, sends)]
    half = channels // 2
    (tok_grads,) = call(
        functools.partial(tokens_kernel, n),
        "tokens",
        [((2 * width, toks), BF16)],
        (sums[2], score_grads, q_turned, g_turned, *norms),
        3,
        limit=LIM_G << 20,
    )
    piece = half // n
    weights = call(
        functools.partial(weights_kernel, n),
        "weights",
        [((half, 2 * width), F32), ((piece + 16, 2 * width), I16)]
        + [((piece, 2 * width), I16)] * (GIVES - 2)
        + [(((n - GIVES + 1) * piece, 2 * width), I16)],
        (inputs, tok_grads, slope_terms),
        1,
        [pltpu.VMEM((2, half, 2 * width), F32)],
        limit=LIM_G << 20,
    )
    got = [swap(x, "dp", 1, 2) for x in weights[1:]]
    latents = call(
        functools.partial(latents_kernel, n, heads),
        "latents",
        [((1, rows, width), BF16)] * 2,
        (sums[1], own_dq, *blocks, *norms),
        1,
    )
    pair = call(
        functools.partial(pair_kernel, n, heads),
        "pair",
        [((piece + 8, 2 * width), F32)] + [((heads * piece + 16, 2 * HEAD), I16)] * (n - 1),
        (weights[0], slope_terms, *got, blocks[0]),
        0.3,
    )
    parts = [swap(pair[k], "seq", k, n) for k in peers]
    last = call(
        functools.partial(last_kernel, n, heads),
        "last",
        [((piece, width), F32), ((piece, width), F32), ((heads,), F32)],
        (pair[0], *parts),
        1,
        out_specs=[VMEM] * 2 + [SMEM],
    )
    return (*latents, *last)


def carried_in(part, axis, combine, identity):
    place = lax.axis_index(axis)
    gathered = lax.all_gather(part, axis)
    state = jnp.zeros_like(part) + jnp.asarray(identity, part.dtype)

    def one(step, state):
        return combine(state, lax.dynamic_index_in_dim(gathered, step, 0, False))

    return lax.fori_loop(0, place, one, state)


def add_counts(earlier, later):
    return earlier + later


def per_device_general(tokens, levels, boundaries, level_table, w_key, w_value, slopes, queries, cotangent):
    scale = HEAD ** (-0.5)
    raw = tokens[0].astype(jnp.float32)
    centered = raw - jnp.mean(raw, axis=1, keepdims=True)
    normed = centered / jnp.sqrt(jnp.mean(centered * centered, axis=1, keepdims=True) + 1e-05)
    lookup = jnp.take(level_table, levels[0], axis=0)
    inputs = (normed + lookup).astype(jnp.bfloat16)
    keys = jnp.dot(inputs, w_key, preferred_element_type=jnp.float32).astype(jnp.bfloat16)
    values = jnp.dot(inputs, w_value, preferred_element_type=jnp.float32).astype(jnp.bfloat16)
    bounds = boundaries[0]
    has = (bounds < BLOCK).astype(jnp.int32)
    earlier = carried_in(jnp.sum(has).reshape(1), "seq", add_counts, jnp.zeros((1,), jnp.int32))
    before = earlier[0] + jnp.cumsum(has) - has
    position = jnp.arange(BLOCK, dtype=jnp.int32)
    inside = (position[None, :] >= bounds[:, None]).astype(jnp.int32)
    episode = (before[:, None] + inside).reshape(-1).astype(jnp.float32)
    query_all, grad_all = (
        lax.all_gather(queries[0], "seq", axis=0, tiled=True),
        lax.all_gather(cotangent[0], "seq", axis=0, tiled=True),
    )
    latents = query_all.shape[0]
    heads = w_key.shape[1] // HEAD
    tok_rows = keys.shape[0]
    own_rows = queries.shape[1]
    start = lax.axis_index("seq") * own_rows
    query_heads = query_all.reshape(latents, heads, HEAD)
    grad_heads = grad_all.reshape(latents, heads, HEAD)
    key_heads = keys.reshape(tok_rows, heads, HEAD)
    value_heads = values.reshape(tok_rows, heads, HEAD)
    score = (
        jnp.einsum("nhd,thd->hnt", query_heads, key_heads, preferred_element_type=jnp.float32)
        * scale
    )
    score = score + slopes[:, None, None] * episode[None, None, :]
    top = lax.pmax(jnp.max(score, axis=2), "seq")
    expo = jnp.exp(score - top[:, :, None])
    part_norm = jnp.sum(expo, axis=2)
    part_out = jnp.einsum(
        "hnt,thd->nhd", expo.astype(jnp.bfloat16), value_heads, preferred_element_type=jnp.float32
    ).reshape(latents, heads * HEAD)
    grad_f32 = grad_all.astype(jnp.float32)
    summed, total = lax.psum((part_out, part_norm), "seq")
    mixed = (summed.reshape(latents, heads, HEAD) / total.T[:, :, None]).reshape(
        latents, heads * HEAD
    )
    delta = jnp.sum((grad_f32 * mixed).reshape(latents, heads, HEAD), axis=2).T
    own_mixed = lax.dynamic_slice_in_dim(mixed, start, own_rows, 0)
    attended = own_mixed.astype(jnp.bfloat16)[None]
    probs = expo / total[:, :, None]
    probs_b = probs.astype(jnp.bfloat16)
    value_tok = (
        jnp.einsum("hnt,nhd->thd", probs_b, grad_heads, preferred_element_type=jnp.float32)
        .astype(jnp.bfloat16)
        .reshape(tok_rows, heads * HEAD)
    )
    dprod = jnp.einsum("nhd,thd->hnt", grad_heads, value_heads, preferred_element_type=jnp.float32)
    score_grad = probs * (dprod - delta[:, :, None])
    slope_part = jnp.sum(score_grad * episode[None, None, :], axis=(1, 2))
    score_grad_b = score_grad.astype(jnp.bfloat16)
    query_part = (
        scale
        * jnp.einsum("hnt,thd->nhd", score_grad_b, key_heads, preferred_element_type=jnp.float32)
    ).reshape(latents, heads * HEAD)
    key_tok = (
        (
            scale
            * jnp.einsum(
                "hnt,nhd->thd", score_grad_b, query_heads, preferred_element_type=jnp.float32
            )
        )
        .astype(jnp.bfloat16)
        .reshape(tok_rows, heads * HEAD)
    )
    query_grad = lax.psum_scatter(query_part, "seq", scatter_dimension=0, tiled=True).astype(
        jnp.bfloat16
    )[None]
    key_part = jnp.dot(inputs.T, key_tok, preferred_element_type=jnp.float32)
    value_part = jnp.dot(inputs.T, value_tok, preferred_element_type=jnp.float32)
    key_weight_grad, value_weight_grad = (
        lax.psum_scatter(key_part, ("dp", "seq"), scatter_dimension=0, tiled=True),
        lax.psum_scatter(value_part, ("dp", "seq"), scatter_dimension=0, tiled=True),
    )
    slope_grad = lax.psum(slope_part, ("dp", "seq"))
    return (attended, query_grad, key_weight_grad, value_weight_grad, slope_grad)


def solution(mesh):
    n = mesh.shape["seq"]

    def per_device(*args):
        toks, (rows, width) = args[0].shape[1], args[7].shape[1:]
        fits = rows % 128 == 0 and toks % CHUNK == 0 and toks // BLOCK <= 256 and width // HEAD <= 4
        if n in (2, 4, 8) and mesh.shape["dp"] == 2 and fits:
            return per_device_blocks(n, *args)
        return per_device_general(*args)

    return jax.shard_map(
        per_device,
        mesh=mesh,
        in_specs=(
            P("dp", "seq", None),
            P("dp", "seq"),
            P("dp", "seq"),
            P(),
            P(None, "tensor"),
            P(None, "tensor"),
            P("tensor"),
            P("dp", "seq", "tensor"),
            P("dp", "seq", "tensor"),
        ),
        out_specs=(
            P("dp", "seq", "tensor"),
            P("dp", "seq", "tensor"),
            P(("dp", "seq"), "tensor"),
            P(("dp", "seq"), "tensor"),
            P("tensor"),
        ),
        check_vma=False,
    )
```
